512 devices in a mesh: pool: 16 (over z_lo, y), tp: 32 (over x, z_hi, core).
Axes of the slice: x: 4, y: 8, z: 8 (z_hi: 4, z_lo: 2; z = z_hi * 2 + z_lo), core: 2. Of those that a mesh axis runs over, the one named last changes fastest.
Arguments:
- page_store: bfloat16 [8192, 64, 576], P(('pool', 'tp')), may hold values from -6.5 to 6.5
- page_table: int32 [128, 64], replicated, may hold values from 0 to 8191, as said below
- context_len: int32 [128], replicated, may hold values from 1 to 4096, 393216 in all
- absorbed_query: bfloat16 [128, 64, 576], P('pool', 'tp'), may hold values from -8 to 8
- value_up: bfloat16 [64, 512, 128], P('tp'), may hold values from -0.25 to 0.25
- out_proj: bfloat16 [8192, 7168], P('tp', 'pool'), may hold values from -0.0625 to 0.0625
Outputs:
- attn_output: bfloat16 [128, 7168], P('tp', 'pool')
The draws below stay inside these ranges and needn't reach their ends.
Inputs may be any that keep to these rules, and one draw needn't show every extreme that they name: `page_table`: every slot of page_store is named exactly once. The 16 slots held by one device of pool+tp name exactly 1 pages of requests of each decode group (requests g * 8 to (g + 1) * 8 - 1 form group g). Page j of request g * 8 + i has q = i * 64 + j and lies in a slot of a device whose tp index is q // 16.
All inputs are finite; a program needn't handle non-finite values.
Results may differ from the reference program's by a relative error of at most 0.015.
Values may be sent and summed in bfloat16 or wider, within the bound.
A program may use at most 128 MiB of HBM per device.

```python
import math
import jax
import jax.numpy as jnp
import numpy as np
from jax import lax

D = 7168
HEADS = 64
LAT = 512
VH = 128
PAGE = 64
CTX = 4096
REQ_GRP = 8
KD = 576
PAGES_REQ = 64
REQ = 128
STORE = 8192
PG_DEV = 16
PER = 1
HV = 8192
N_POOL = 16
N_TP = 32


def draw_page_table(key, part):
    key = jax.random.fold_in(key, 11)
    group_pages = REQ_GRP * PAGES_REQ
    device_count = N_POOL * N_TP
    block_keys = jax.random.split(jax.random.fold_in(key, 1), N_POOL * N_TP)
    block_order = jax.vmap(lambda piece_key: jax.random.permutation(piece_key, PG_DEV))(block_keys)
    block_order = block_order.reshape(N_POOL, N_TP, PG_DEV)
    device_keys = jax.random.split(jax.random.fold_in(key, 2), device_count)
    local_order = jax.vmap(lambda piece_key: jax.random.permutation(piece_key, PG_DEV))(device_keys)
    placed = jnp.arange(group_pages, dtype=jnp.int32)
    tp_block = placed // PG_DEV
    inside = placed % PG_DEV
    groups = jnp.arange(N_POOL, dtype=jnp.int32)
    ranked = block_order[groups[:, None], tp_block[None, :], inside[None, :]]
    source_pool = ranked // PER
    within = ranked % PER
    holder = source_pool * N_TP + tp_block[None, :]
    local_slot = local_order[holder, groups[:, None] * PER + within]
    table = (holder * PG_DEV + local_slot).astype(jnp.int32)
    return table.reshape(REQ, PAGES_REQ)


def draw_page_store(key, part):
    key = jax.random.fold_in(key, 21)
    shape = (STORE, PAGE, KD)
    values = jax.random.truncated_normal(key, -6.0, 6.0, shape, jnp.float32)
    return values.astype(jnp.bfloat16)


def draw_absorbed_query(key, part):
    key = jax.random.fold_in(key, 31)
    shape = (REQ, HEADS, KD)
    values = 1.3 * jax.random.truncated_normal(key, -6.0, 6.0, shape, jnp.float32)
    return values.astype(jnp.bfloat16)


def level_of(stream_key, dims, pieces, low, largest):
    factor_of, own = 1.0, jax.random.fold_in(stream_key, 6)
    for position, parts in pieces:
        steps = jnp.exp(jax.random.uniform(jax.random.fold_in(own, position), (parts,), jnp.float32, low / len(pieces), largest / len(pieces)))
        factor_of = factor_of * jnp.repeat(steps, dims[position] // parts).reshape([-1 if axis == position else 1 for axis in range(len(dims))])
    return factor_of


def profile(count, total, most, skew):
    loads = [(1 << 20) // math.isqrt(grade ** skew) + 1 for grade in range(2, count + 1)]
    spare, given = total - most - (count - 1), [1] * (count - 1)
    while spare > 0:
        movable = [i for i in range(count - 1) if given[i] < most]
        pool, remaining = sum([loads[i] for i in movable]), spare
        for i in movable:
            extra = min(most - given[i], max(1, remaining * loads[i] // pool), spare)
            given[i] = given[i] + extra
            spare = spare - extra
    return np.array([most] + given)


def uneven(own_key, count, total, most, skew):
    if count == 2:
        one = jax.random.randint(own_key, (), max(1, total - most), min(most, total - 1) + 1)
        return jnp.stack([one, total - one])
    lengths = jnp.asarray(profile(count, total, most, skew), jnp.int32)
    pairs = (count - 1) // 2
    giver, receiver = lengths[1:1 + 2 * pairs:2], lengths[2:2 + 2 * pairs:2]
    slack = jnp.minimum(giver - 1, most - receiver)
    passed = jax.random.randint(jax.random.fold_in(own_key, 1), (pairs,), 0, 1 << 20) % (slack + 1)
    lengths = lengths.at[1:1 + 2 * pairs:2].set(giver - passed).at[2:2 + 2 * pairs:2].set(receiver + passed)
    return lengths[jax.random.permutation(jax.random.fold_in(own_key, 2), count)]


def noise(key, extent, scale, bound, pieces=(), kind=jnp.bfloat16):
    entries = jax.random.normal(key, extent, jnp.float32) * scale
    if len(pieces) > 0:
        entries = level_of(key, extent, pieces, -0.22, 0.18) * entries
    return jnp.clip(entries, min=-bound, max=bound).astype(kind)


def setup_inputs(seed: int = 0) -> dict:
    streams_of = jax.random.split(jax.random.key(seed), 7)
    return {
        "page_store": draw_page_store(jax.random.fold_in(streams_of[6], 71), 0),
        "page_table": draw_page_table(jax.random.fold_in(streams_of[6], 71), 0),
        "context_len": uneven(streams_of[2], REQ, REQ * CTX * 3 // 4, CTX, 1).astype(jnp.int32),
        "absorbed_query": draw_absorbed_query(jax.random.fold_in(streams_of[6], 71), 0),
        "value_up": noise(streams_of[4], (HEADS, LAT, VH), LAT ** -0.5, 0.25, ((0, 32),)),
        "out_proj": noise(streams_of[5], (HV, D), HV ** -0.5, 0.0625, ((0, 32), (1, 16))),
    }


score_scale = 192.0 ** -0.5
masked_score = -1.0e30


def reference(page_store, page_table, context_len, absorbed_query, value_up, out_proj):
    key_width = page_store.shape[2]
    page_tokens = page_store.shape[1]
    latent_width = value_up.shape[1]

    def attend_request(request_index):
        page_slots = page_table[request_index]
        key_pages = jnp.take(page_store, page_slots, axis=0)
        page_count = key_pages.shape[0]
        scores = jnp.einsum("hk,pik->hpi", absorbed_query[request_index].astype(jnp.float32),
                            key_pages.astype(jnp.float32))
        positions = (jnp.arange(page_count, dtype=jnp.int32)[:, None] * page_tokens
                     + jnp.arange(page_tokens, dtype=jnp.int32)[None, :])
        usable = positions < context_len[request_index]
        scores = jnp.where(usable[None], scores * score_scale, masked_score)
        page_top = jnp.max(scores, axis=-1)
        weights = jnp.where(usable[None], jnp.exp(scores - page_top[..., None]), 0.0)
        page_total = jnp.sum(weights, axis=-1)
        page_mixed = jnp.einsum("hpi,pil->hpl", weights.astype(jnp.bfloat16).astype(jnp.float32),
                                key_pages[:, :, :latent_width].astype(jnp.float32))
        row_top = jnp.max(page_top, axis=-1)
        factor = jnp.exp(page_top - row_top[:, None])
        weight_total = jnp.sum(factor * page_total, axis=-1)
        mixed = jnp.sum(factor[..., None] * page_mixed, axis=1)
        attended = (mixed / weight_total[:, None]).astype(jnp.bfloat16)
        head_output = jnp.einsum("hl,hlv->hv", attended.astype(jnp.float32), value_up.astype(jnp.float32))
        return head_output.astype(jnp.bfloat16).reshape(-1)

    all_requests = lax.map(attend_request, jnp.arange(absorbed_query.shape[0], dtype=jnp.int32))
    return jnp.dot(all_requests, out_proj, preferred_element_type=jnp.float32).astype(jnp.bfloat16)
```

```python
import functools
import itertools

import jax
import jax.numpy as jnp
from jax import lax
from jax.experimental import pallas as pl
from jax.experimental.pallas import tpu as pltpu
from jax.sharding import PartitionSpec as P

MESH = pl.DeviceIdType.MESH
score_scale = 192.0 ** (-0.5)
masked_score = -1e30
F32 = jnp.float32
BF16 = jnp.bfloat16
LANES = 128
MSG = 16
CHUNK = 4
FAR = 3
SITE = 8
PIECES = 1
X_CORE = [(2, 1), (2, 0), (1, 1), (3, 1), (1, 0), (3, 0), (0, 1)]
Z_HI = [2, 1, 3]
TP = [(dz, dx, dc) for dz in (2, 1, 3, 0) for dx in (2, 1, 3, 0) for dc in (1, 0)][:-1]
POOL = [(dz, dy) for dy in (4, 3, 5, 2, 6, 1, 7) for dz in (1, 0)] + [(1, 0)]
SITES = [(dz, dy) for dz, dy in POOL if dy not in (3, 4, 5)]
QUARTERS = 4
GROUPS = 8
BLOCKS = 5


def split3(x):
    hi = x.astype(BF16).astype(F32)
    mid = (x - hi).astype(BF16).astype(F32)
    return hi, mid, x - hi - mid


def each(first, last, body):
    def step(i, carry):
        body(i)
        return carry

    lax.fori_loop(first, last, step, 0)


def kernel(
    n_pool,
    n_tp,
    table_hbm,
    len_hbm,
    store_hbm,
    query_hbm,
    up_hbm,
    proj_hbm,
    out_ref,
    table_ref,
    len_ref,
    store_ref,
    query_ref,
    up_ref,
    proj_ref,
    local_sem,
    stage,
    land,
    q_msg,
    q_land,
    q_part,
    q_all,
    far_msg,
    far_land,
    part_msg,
    part_land,
    head_msg,
    head_land,
    last_msg,
    wide,
    top_ref,
    total_ref,
    mixed_ref,
    page_send,
    page_recv,
    q_send,
    q_recv,
    all_send,
    all_recv,
    part_send,
    part_recv,
    head_send,
    head_recv,
    last_send,
    last_recv,
):
    pool = lax.axis_index("pool")
    tp = lax.axis_index("tp")
    n_y = n_pool // 2
    z, y = pool // n_y, pool % n_y
    sign = 1 - 2 * z
    page_tokens = store_ref.shape[1]
    requests = query_ref.shape[0]
    request, quarter = tp // QUARTERS, tp % QUARTERS
    x, z_hi, core = tp // 8, tp // 2 % 4, tp % 2
    first_page = quarter * n_pool

    def place(at_z, at_y):
        return at_z * n_y + (at_y + 2 * n_y) % n_y

    def across(step):
        dx, dc = step
        return (x + dx) % 4 * 2 + (core + dc) % 2

    def along(dz):
        return (z_hi + dz) % 4

    def tp_of(step):
        dz, dx, dc = step
        return (x + dx) % 4 * 8 + (z_hi + dz) % 4 * 2 + (core + dc) % 2

    def pool_of(step):
        dz, dy = step
        return (z + dz) % 2 * n_y + (y + dy) % n_y

    def number(step):
        return step[0] * 8 + (step[1] if len(step) == 2 else step[1] * 2 + step[2])

    def to(tp_index, pool_index=pool):
        return {"pool": pool_index, "tp": tp_index}

    barrier = pltpu.get_barrier_semaphore()
    loads = [
        pltpu.make_async_copy(source, target, local_sem.at[i])
        for i, (source, target) in enumerate(
            [
                (query_hbm, query_ref),
                (table_hbm.at[pl.ds(pl.multiple_of(first_page, 8), n_pool)], table_ref),
                (store_hbm, store_ref),
                (len_hbm, len_ref),
                (up_hbm, up_ref),
                (proj_hbm, proj_ref),
            ]
        )
    ]
    for load in loads[:3]:
        load.start()

    def greet(tp_index, pool_index=pool):
        device = to(tp_index, pool_index)
        pl.semaphore_signal(barrier, inc=1, device_id=device, device_id_type=MESH)

    for step in X_CORE:
        greet(tp_of((0, *step)))
    for step in SITES:
        greet(tp, pool_of(step))
    for ahead in (FAR, -FAR):
        for dz in Z_HI + [0]:
            greet(tp_of((dz, 0, 0)), place(z, y + ahead))
    for dz in Z_HI:
        greet(tp_of((dz, 0, 0)))
    greetings = len(X_CORE) + len(SITES) + 2 * QUARTERS + len(Z_HI)
    for load in loads[3:]:
        load.start()

    me = pool * n_tp + tp

    def slot_of(group):
        row = group * requests + request

        def look(k, found):
            entry = table_ref[k, row]
            return found + jnp.where(entry >> 4 == me, entry & 15, 0)

        return lax.fori_loop(0, n_pool, look, 0, unroll=True)

    half = page_tokens // 2

    def packed(target, slot):
        for c in range(4):
            target[c * page_tokens : (c + 1) * page_tokens] = store_ref[
                slot, :, c * LANES : (c + 1) * LANES
            ]
        rest = store_ref[slot, :, 4 * LANES :]
        target[4 * page_tokens :] = jnp.concatenate([rest[:half], rest[half:]], axis=1)

    def remote(source, target, sems, i, device):
        send, recv = sems
        return pltpu.make_async_remote_copy(
            src_ref=source,
            dst_ref=target,
            send_sem=send.at[i],
            recv_sem=recv.at[i],
            device_id=device,
            device_id_type=MESH,
        )

    def start(copies):
        for copy in copies:
            copy.start()

    def arrive(copies):
        for copy in copies:
            copy.wait_recv()

    def route(n):
        k = n % 4
        return 1 - n // 4, (6 + k + n // 4 * (k // 2) * (6 * k - 11)) % n_y

    piece_rows = stage.shape[1] // PIECES

    def page_copy(role, n, rows=slice(None)):
        dz, move = route(n)
        to_z = (z + dz) % 2
        direction = (1 - 2 * to_z) * (1 - 2 * role)
        return remote(
            stage.at[role * SITE + n, rows],
            land.at[role * SITE + n, rows],
            (page_send, page_recv),
            role * SITE + n,
            to(tp, to_z * n_y + (y + direction * move + n_y) % n_y),
        )

    def send_pages(role, first, last):
        def send(i):
            n = (i + core * (SITE // 2)) % SITE
            dz, move = route(n)
            to_z = (z + dz) % 2
            direction = 1 - 2 * to_z
            ahead = direction * (1 - 2 * role) * move - direction * (1 - role) * FAR
            packed(stage.at[role * SITE + n], slot_of(to_z * n_y + (y + ahead + 2 * n_y) % n_y))

            @pl.when(n < SITE - 1)
            def _():
                for piece in range(PIECES):
                    page_copy(role, n, pl.ds(piece * piece_rows, piece_rows)).start()

        each(first, last, send)
        if last == SITE:
            local = role * SITE + SITE - 1
            land[local] = stage[local]

    loads[0].wait()
    for i in range(requests):
        for c in range(BLOCKS):
            width = min(LANES, query_ref.shape[-1] - c * LANES)
            wide[i * MSG + 2 * c : i * MSG + 2 * c + 2, :width] = query_ref[
                i, :, c * LANES : c * LANES + width
            ].astype(F32)
        wide[i * MSG + 2 * BLOCKS - 2 : (i + 1) * MSG, LANES // 2 :] = jnp.zeros((8, LANES // 2), F32)
        wide[i * MSG + 2 * BLOCKS : (i + 1) * MSG, : LANES // 2] = jnp.zeros((6, LANES // 2), F32)
    q_msg[...] = wide[: requests * MSG].astype(BF16).reshape(q_msg.shape)

    here = x * 2 + core

    def q_copy(step):
        peer = across(step)
        return remote(
            q_msg.at[pl.ds(peer // 2 * 2, 2)],
            q_land.at[here],
            (q_send, q_recv),
            number(step),
            to(tp_of((0, *step))),
        )

    pl.semaphore_wait(barrier, greetings)
    start(map(q_copy, X_CORE))
    loads[1].wait()
    loads[2].wait()
    send_pages(0, 0, SITE // 2)

    q_land[here] = q_msg[pl.ds(x * 2, 2)]
    arrive(map(q_copy, X_CORE))
    wide[: 2 * SITE * MSG] = q_land[...].reshape(2 * SITE * MSG, LANES).astype(F32)
    for i, c in itertools.product(range(2), range(BLOCKS)):
        halves = [wide[pl.ds(i * MSG + 2 * c + e, SITE, stride=2 * MSG), :] for e in range(2)]
        q_part[i, c] = jnp.concatenate(halves, axis=0).astype(BF16)

    def query_copy(role, dz):
        return remote(
            q_part.at[along(dz) // 2],
            q_all.at[role, z_hi],
            (all_send, all_recv),
            role * QUARTERS + dz,
            to(tp_of((dz, 0, 0)), z * n_y + (y + (1 - role) * sign * FAR + n_y) % n_y),
        )

    def part_copy(step):
        peer = tp_of(step)
        held = along(step[0]) * 8 + across(step[1:])
        return remote(
            part_msg.at[held], part_land.at[tp], (part_send, part_recv), number(step), to(peer)
        )

    def back_copy(rows=slice(None)):
        return remote(
            far_msg.at[rows], far_land.at[rows], (all_send, all_recv), 2 * QUARTERS, to(tp, place(z, y - sign * FAR))
        )

    start([query_copy(0, dz) for dz in Z_HI + [0]])
    start([query_copy(1, dz) for dz in Z_HI])
    q_all[1, z_hi] = q_part[z_hi // 2]
    send_pages(0, SITE // 2, SITE)
    send_pages(1, 0, SITE)
    for load in loads[3:]:
        load.wait()

    lat = up_ref.shape[1]
    heads = 2 * n_tp
    transposed = (((1,), (1,)), ((), ()))

    tokens = CHUNK * page_tokens

    def attend(step):
        role, part = step // 2, (step + core) % 2
        group = z * n_y + (y - sign * (1 - role) * FAR + n_y) % n_y
        row = group * requests + request
        length = len_ref[row]

        @pl.when(step % 2 == 0)
        def _():
            top_ref[...] = jnp.full(top_ref.shape, masked_score, F32)
            total_ref[...] = jnp.zeros(total_ref.shape, F32)
            mixed_ref[...] = jnp.zeros(mixed_ref.shape, F32)
            arrive([query_copy(role, dz) for dz in Z_HI])

            @pl.when(role == 0)
            def _():
                query_copy(0, 0).wait_recv()

        lane = lax.broadcasted_iota(jnp.int32, (1, tokens), 1)
        n = part * CHUNK + lane % (CHUNK * half) // half
        dz, move = route(n)
        source = (z + dz) % 2 * n_y + (y - sign * (1 - 2 * role) * move + n_y) % n_y
        limit = jnp.zeros_like(lane)
        for k in range(n_pool):
            holder = table_ref[k, row] >> 9
            limit = jnp.where(source == holder, length - (first_page + k) * page_tokens, limit)
        live = lane // (CHUNK * half) * half + lane % half < limit

        blocks = [
            jnp.concatenate([q_all[role, u, c] for u in range(QUARTERS)], axis=0)
            for c in range(BLOCKS)
        ]
        query = jnp.concatenate(blocks[:4], axis=1)
        rest = blocks[4][:, : LANES // 2]
        blank = jnp.zeros_like(rest)
        rest = jnp.concatenate(
            [jnp.concatenate([rest, blank], axis=1), jnp.concatenate([blank, rest], axis=1)], axis=0
        )
        first = part * CHUNK
        each(first, first + CHUNK - part, lambda n: page_copy(role, n).wait_recv())
        block = land[pl.ds(role * SITE + first, CHUNK)]

        def rows(begin):
            return block[:, begin : begin + half].reshape(CHUNK * half, LANES)

        keys = jnp.concatenate(
            [
                jnp.concatenate([rows(c * page_tokens + h * half) for c in range(4)], axis=1)
                for h in range(2)
            ],
            axis=0,
        )
        scores = lax.dot_general(query, keys, transposed, preferred_element_type=F32)
        extra = lax.dot_general(rest, rows(4 * page_tokens), transposed, preferred_element_type=F32)
        scores += jnp.concatenate([extra[:heads], extra[heads:]], axis=1)
        scores = jnp.where(live, scores * score_scale, masked_score)
        top = top_ref[...]
        new_top = jnp.maximum(top, jnp.max(scores, axis=1, keepdims=True))
        weights = jnp.where(live, jnp.exp(scores - new_top[:, :1]), 0.0)
        scale = jnp.exp(top - new_top)
        total = total_ref[...] * scale + jnp.sum(weights, axis=1, keepdims=True)
        update = jnp.dot(weights.astype(BF16), keys, preferred_element_type=F32)
        mixed = mixed_ref[...] * scale[:, :1] + update
        top_ref[...] = new_top
        total_ref[...] = total
        mixed_ref[...] = mixed

        @pl.when(step == 1)
        def _():
            lse, even = normalised(new_top, total, mixed)
            for c in range(4):
                far_msg[c * heads : (c + 1) * heads] = even[:, c * LANES : (c + 1) * LANES].astype(BF16)
            lane = lax.broadcasted_iota(jnp.int32, (heads, LANES), 1)
            hi, mid, low = split3(lse)
            stat = jnp.where(lane == 0, hi, jnp.where(lane == 1, mid, jnp.where(lane == 2, low, 0.0)))
            far_msg[4 * heads :] = stat.astype(BF16)
            start([back_copy(pl.ds(c * heads, heads)) for c in range(BLOCKS)])

    def normalised(top, total, mixed):
        some = total > 0.0
        safe = jnp.where(some, total, 1.0)
        inverse = 1.0 / safe
        return jnp.where(some, top + jnp.log(safe), masked_score), mixed * inverse[:, :1]

    each(0, 4, attend)
    back_copy().wait_recv()
    back = jnp.sum(far_land[4 * heads :].astype(F32), axis=1, keepdims=True)
    top = top_ref[...]
    new_top = jnp.maximum(top, back)
    scale = jnp.exp(top - new_top)
    share = jnp.where(back > 0.5 * masked_score, jnp.exp(back - new_top), 0.0)
    mixed = jnp.concatenate(
        [
            mixed_ref[:, c * LANES : (c + 1) * LANES] * scale
            + far_land[c * heads : (c + 1) * heads].astype(F32) * share
            for c in range(4)
        ],
        axis=1,
    )
    lse, even = normalised(new_top, total_ref[...] * scale + share, mixed)
    parts = split3(lse) + (jnp.zeros_like(lse),)
    for u, e in itertools.product(range(QUARTERS), range(2)):
        mine = slice(u * MSG + e * 8, u * MSG + e * 8 + 8)
        for c in range(4):
            row = u * 8 * MSG + 2 * c + e
            wide[pl.ds(row, 8, stride=MSG), :] = even[mine, c * LANES : (c + 1) * LANES]
            wide[pl.ds(row + 8, 8, stride=MSG), :] = parts[c][mine]
    part_msg[...] = wide[...].astype(BF16).reshape(part_msg.shape)
    part_copies = [part_copy(step) for step in TP]
    start(part_copies)
    part_land[tp] = part_msg[z_hi * 8 + here]
    arrive(part_copies)

    wide[...] = part_land[...].reshape(wide.shape).astype(F32)
    values = []
    for e in range(2):

        def rows(k, j):
            return wide[pl.ds(k * MSG + 2 * j + e, GROUPS, stride=QUARTERS * MSG), :]

        lses = [rows(k, 4) + rows(k, 5) + rows(k, 6) for k in range(QUARTERS)]
        best = functools.reduce(jnp.maximum, lses)
        share = [jnp.exp(one - best) for one in lses]
        norm = 1.0 / functools.reduce(jnp.add, share)
        attended = []
        for c in range(4):
            block = functools.reduce(jnp.add, [share[k] * rows(k, c) for k in range(QUARTERS)])
            attended.append((block * norm).astype(BF16))
        attended = jnp.concatenate(attended, axis=1)
        values.append(jnp.dot(attended, up_ref[e], preferred_element_type=F32))
    head_msg[...] = jnp.concatenate(values, axis=0).astype(BF16)

    def head_copy(step):
        return remote(
            head_msg, head_land.at[pool], (head_send, head_recv), number(step), to(tp, pool_of(step))
        )

    start(map(head_copy, POOL))
    head_land[pool] = head_msg[...]
    arrive(map(head_copy, POOL))

    landed = head_land[...].astype(F32)
    left = [landed[:, 8 * e : 8 * e + 8].reshape(4 * n_tp, LANES).astype(BF16) for e in range(2)]
    product = lax.dot_general(
        jnp.concatenate(left, axis=1), proj_ref[...], transposed, preferred_element_type=F32
    )
    columns = proj_ref.shape[0]
    blank = jnp.zeros((4 * n_tp, 4 * LANES - columns), F32)
    product = jnp.concatenate([product, blank], axis=1)
    for j in range(n_tp):
        last_msg[j] = product[4 * j : 4 * j + 4].astype(BF16)

    def last_copy(step):
        peer = tp_of(step)
        return remote(
            last_msg.at[peer], out_ref.at[tp], (last_send, last_recv), number(step), to(peer)
        )

    start(map(last_copy, TP))
    own = pltpu.make_async_copy(last_msg.at[tp], out_ref.at[tp], last_send.at[0])
    own.start()
    each(0, SITE - 1, lambda n: page_copy(0, n).wait_send())
    each(0, SITE - 1, lambda n: page_copy(1, n).wait_send())
    sent = [q_copy(step) for step in X_CORE]
    sent += [query_copy(0, dz) for dz in Z_HI + [0]] + [query_copy(1, dz) for dz in Z_HI]
    sent += [back_copy()] + part_copies
    sent += [head_copy(step) for step in POOL]
    sent += [last_copy(step) for step in TP]
    for copy in sent:
        copy.wait_send()
    own.wait()
    arrive(map(last_copy, TP))


def per_device(n_pool, n_tp, page_store, page_table, context_len, absorbed_query, value_up, out_proj):
    pages, tokens, key_width = page_store.shape
    requests = absorbed_query.shape[0]
    columns = out_proj.shape[1]
    hbm = pl.BlockSpec(memory_space=pltpu.HBM)
    message = lambda *lead: pltpu.VMEM((*lead, MSG, LANES), BF16)
    sems = lambda n: [pltpu.SemaphoreType.DMA((n,)), pltpu.SemaphoreType.DMA((n,))]
    summands = pl.pallas_call(
        functools.partial(kernel, n_pool, n_tp),
        out_shape=jax.ShapeDtypeStruct((n_tp, 4, 4 * LANES), BF16),
        in_specs=[hbm] * 6,
        out_specs=hbm,
        scratch_shapes=[
            pltpu.SMEM((n_pool, page_table.shape[0]), jnp.int32),
            pltpu.SMEM(context_len.shape, jnp.int32),
            pltpu.VMEM(page_store.shape, BF16),
            pltpu.VMEM(absorbed_query.shape, BF16),
            pltpu.VMEM(value_up.shape, BF16),
            pltpu.VMEM(out_proj.shape[::-1], BF16),
            pltpu.SemaphoreType.DMA((6,)),
            pltpu.VMEM((n_pool, tokens * key_width // LANES, LANES), BF16),
            pltpu.VMEM((n_pool, tokens * key_width // LANES, LANES), BF16),
            message(GROUPS),
            message(SITE, 2),
            message(2, BLOCKS),
            message(2, QUARTERS, BLOCKS),
            pltpu.VMEM((BLOCKS * 2 * n_tp, LANES), BF16),
            pltpu.VMEM((BLOCKS * 2 * n_tp, LANES), BF16),
            message(n_tp),
            message(n_tp),
            message(),
            message(n_pool),
            pltpu.VMEM((n_tp, 4, 4 * LANES), BF16),
            pltpu.VMEM((n_tp * MSG, LANES), F32),
            pltpu.VMEM((2 * n_tp, LANES), F32),
            pltpu.VMEM((2 * n_tp, LANES), F32),
            pltpu.VMEM((2 * n_tp, value_up.shape[1]), F32),
            *sems(2 * SITE),
            *sems(4 * SITE),
            *sems(2 * QUARTERS + 1),
            *sems(n_tp),
            *sems(2 * SITE),
            *sems(n_tp),
        ],
        compiler_params=pltpu.CompilerParams(
            collective_id=0, has_side_effects=True, vmem_limit_bytes=62 * 1024 * 1024
        ),
        name="mla_decode",
    )(page_table.T, context_len, page_store, absorbed_query, value_up, out_proj.T)
    return jnp.sum(summands.astype(F32), axis=0)[:, :columns].astype(BF16)


def solution(mesh):
    placed = (
        P(("pool", "tp"), None, None),
        P(),
        P(),
        P("pool", "tp", None),
        P("tp", None, None),
        P("tp", "pool"),
    )
    return jax.shard_map(
        functools.partial(per_device, mesh.shape["pool"], mesh.shape["tp"]),
        mesh=mesh,
        in_specs=placed,
        out_specs=P("tp", "pool"),
        check_vma=False,
    )
```

```python
import functools
import itertools

import jax
import jax.numpy as jnp
from jax import lax
from jax.experimental import pallas as pl
from jax.experimental.pallas import tpu as pltpu
from jax.sharding import PartitionSpec as P

MESH = pl.DeviceIdType.MESH
score_scale = 192.0 ** (-0.5)
masked_score = -1e30
F32 = jnp.float32
BF16 = jnp.bfloat16
LANES = 128
MSG = 16
CHUNK = 4
FAR = 3
SITE = 8
PIECES = 1
SELF = (0, 0, 0)
X_CORE = [(2, 1), (2, 0), (1, 1), (3, 1), (1, 0), (3, 0), (0, 1)]
Z_HI = [2, 1, 3]
TP = [(dz, dx, dc) for dz in (2, 1, 3, 0) for dx in (2, 1, 3, 0) for dc in (1, 0)][:-1]
POOL = [(dz, dy) for dy in (4, 3, 5, 2, 6, 1, 7) for dz in (1, 0)] + [(1, 0)]
SITES = [(dz, dy) for dz, dy in POOL if dy not in (3, 4, 5)]
QUARTERS = 4
GROUPS = 8
BLOCKS = 5


def split3(x):
    hi = x.astype(BF16).astype(F32)
    mid = (x - hi).astype(BF16).astype(F32)
    return hi, mid, x - hi - mid


def each(first, last, body):
    def step(i, carry):
        body(i)
        return carry

    lax.fori_loop(first, last, step, 0)


def kernel(
    n_pool,
    n_tp,
    table_hbm,
    len_hbm,
    store_hbm,
    query_hbm,
    up_hbm,
    proj_hbm,
    out_ref,
    table_ref,
    len_ref,
    store_ref,
    query_ref,
    up_ref,
    proj_ref,
    local_sem,
    stage,
    land,
    q_msg,
    q_land,
    q_part,
    q_all,
    part_msg,
    part_land,
    head_msg,
    head_land,
    last_msg,
    wide,
    top_ref,
    total_ref,
    mixed_ref,
    page_send,
    page_recv,
    q_send,
    q_recv,
    all_send,
    all_recv,
    part_send,
    part_recv,
    head_send,
    head_recv,
    last_send,
    last_recv,
):
    pool = lax.axis_index("pool")
    tp = lax.axis_index("tp")
    n_y = n_pool // 2
    z, y = pool // n_y, pool % n_y
    sign = 1 - 2 * z
    page_tokens = store_ref.shape[1]
    requests = query_ref.shape[0]
    request, quarter = tp // QUARTERS, tp % QUARTERS
    x, z_hi, core = tp // 8, tp // 2 % 4, tp % 2
    first_page = quarter * n_pool

    def place(at_z, at_y):
        return at_z * n_y + (at_y + 2 * n_y) % n_y

    def across(step):
        dx, dc = step
        return (x + dx) % 4 * 2 + (core + dc) % 2

    def along(dz):
        return (z_hi + dz) % 4

    def tp_of(step):
        dz, dx, dc = step
        return (x + dx) % 4 * 8 + (z_hi + dz) % 4 * 2 + (core + dc) % 2

    def pool_of(step):
        dz, dy = step
        return (z + dz) % 2 * n_y + (y + dy) % n_y

    def number(step):
        return step[0] * 8 + (step[1] if len(step) == 2 else step[1] * 2 + step[2])

    def to(tp_index, pool_index=pool):
        return {"pool": pool_index, "tp": tp_index}

    barrier = pltpu.get_barrier_semaphore()
    loads = [
        pltpu.make_async_copy(source, target, local_sem.at[i])
        for i, (source, target) in enumerate(
            [
                (query_hbm, query_ref),
                (table_hbm.at[pl.ds(pl.multiple_of(first_page, 8), n_pool)], table_ref),
                (store_hbm, store_ref),
                (len_hbm, len_ref),
                (up_hbm, up_ref),
                (proj_hbm, proj_ref),
            ]
        )
    ]
    for load in loads[:3]:
        load.start()

    def greet(tp_index, pool_index=pool):
        device = to(tp_index, pool_index)
        pl.semaphore_signal(barrier, inc=1, device_id=device, device_id_type=MESH)

    for step in X_CORE:
        greet(tp_of((0, *step)))
    for step in SITES:
        greet(tp, pool_of(step))
    for ahead in (FAR, -FAR):
        for dz in Z_HI + [0]:
            greet(tp_of((dz, 0, 0)), place(z, y + ahead))
    for dz in Z_HI:
        greet(tp_of((dz, 0, 0)))
    greetings = len(X_CORE) + len(SITES) + 2 * QUARTERS + len(Z_HI)
    for load in loads[3:]:
        load.start()

    me = pool * n_tp + tp

    def slot_of(group):
        row = group * requests + request

        def look(k, found):
            entry = table_ref[k, row]
            return found + jnp.where(entry >> 4 == me, entry & 15, 0)

        return lax.fori_loop(0, n_pool, look, 0, unroll=True)

    half = page_tokens // 2

    def packed(target, slot):
        for c in range(4):
            target[c * page_tokens : (c + 1) * page_tokens] = store_ref[
                slot, :, c * LANES : (c + 1) * LANES
            ]
        rest = store_ref[slot, :, 4 * LANES :]
        target[4 * page_tokens :] = jnp.concatenate([rest[:half], rest[half:]], axis=1)

    def remote(source, target, sems, i, device):
        send, recv = sems
        return pltpu.make_async_remote_copy(
            src_ref=source,
            dst_ref=target,
            send_sem=send.at[i],
            recv_sem=recv.at[i],
            device_id=device,
            device_id_type=MESH,
        )

    def start(copies):
        for copy in copies:
            copy.start()

    def arrive(copies):
        for copy in copies:
            copy.wait_recv()

    def route(n):
        k = n % 4
        return 1 - n // 4, (6 + k + n // 4 * (k // 2) * (6 * k - 11)) % n_y

    piece_rows = stage.shape[1] // PIECES

    def page_copy(role, n, rows=slice(None)):
        dz, move = route(n)
        to_z = (z + dz) % 2
        direction = (1 - 2 * to_z) * (1 - 2 * role)
        return remote(
            stage.at[role * SITE + n, rows],
            land.at[role * SITE + n, rows],
            (page_send, page_recv),
            role * SITE + n,
            to(tp, to_z * n_y + (y + direction * move + n_y) % n_y),
        )

    def send_pages(role, first, last):
        def send(i):
            n = (i + core * (SITE // 2)) % SITE
            dz, move = route(n)
            to_z = (z + dz) % 2
            direction = 1 - 2 * to_z
            ahead = direction * (1 - 2 * role) * move - direction * (1 - role) * FAR
            packed(stage.at[role * SITE + n], slot_of(to_z * n_y + (y + ahead + 2 * n_y) % n_y))

            @pl.when(n < SITE - 1)
            def _():
                for piece in range(PIECES):
                    page_copy(role, n, pl.ds(piece * piece_rows, piece_rows)).start()

        each(first, last, send)
        if last == SITE:
            local = role * SITE + SITE - 1
            land[local] = stage[local]

    loads[0].wait()
    for i in range(requests):
        for c in range(BLOCKS):
            width = min(LANES, query_ref.shape[-1] - c * LANES)
            wide[i * MSG + 2 * c : i * MSG + 2 * c + 2, :width] = query_ref[
                i, :, c * LANES : c * LANES + width
            ].astype(F32)
        wide[i * MSG + 2 * BLOCKS - 2 : (i + 1) * MSG, LANES // 2 :] = jnp.zeros((8, LANES // 2), F32)
        wide[i * MSG + 2 * BLOCKS : (i + 1) * MSG, : LANES // 2] = jnp.zeros((6, LANES // 2), F32)
    q_msg[...] = wide[: requests * MSG].astype(BF16).reshape(q_msg.shape)

    here = x * 2 + core

    def q_copy(step):
        peer = across(step)
        return remote(
            q_msg.at[pl.ds(peer // 2 * 2, 2)],
            q_land.at[here],
            (q_send, q_recv),
            number(step),
            to(tp_of((0, *step))),
        )

    pl.semaphore_wait(barrier, greetings)
    start(map(q_copy, X_CORE))
    loads[1].wait()
    loads[2].wait()
    send_pages(0, 0, SITE // 2)

    q_land[here] = q_msg[pl.ds(x * 2, 2)]
    arrive(map(q_copy, X_CORE))
    wide[: 2 * SITE * MSG] = q_land[...].reshape(2 * SITE * MSG, LANES).astype(F32)
    for i, c in itertools.product(range(2), range(BLOCKS)):
        halves = [wide[pl.ds(i * MSG + 2 * c + e, SITE, stride=2 * MSG), :] for e in range(2)]
        q_part[i, c] = jnp.concatenate(halves, axis=0).astype(BF16)

    def query_copy(role, dz):
        return remote(
            q_part.at[along(dz) // 2],
            q_all.at[role, z_hi],
            (all_send, all_recv),
            role * QUARTERS + dz,
            to(tp_of((dz, 0, 0)), z * n_y + (y + (1 - role) * sign * FAR + n_y) % n_y),
        )

    def part_copy(role, step):
        peer = tp_of(step)
        held = along(step[0]) * 8 + across(step[1:])
        return remote(
            part_msg.at[role, held],
            part_land.at[role, tp],
            (part_send, part_recv),
            role * n_tp + number(step),
            to(peer, z * n_y + (y - (1 - role) * sign * FAR + n_y) % n_y),
        )

    start([query_copy(0, dz) for dz in Z_HI + [0]])
    start([query_copy(1, dz) for dz in Z_HI])
    q_all[1, z_hi] = q_part[z_hi // 2]
    send_pages(0, SITE // 2, SITE)
    send_pages(1, 0, SITE)
    for load in loads[3:]:
        load.wait()

    lat = up_ref.shape[1]
    heads = 2 * n_tp
    transposed = (((1,), (1,)), ((), ()))

    tokens = CHUNK * page_tokens

    def attend(step):
        role, part = step // 2, (step + core) % 2
        group = z * n_y + (y - sign * (1 - role) * FAR + n_y) % n_y
        row = group * requests + request
        length = len_ref[row]

        @pl.when(step % 2 == 0)
        def _():
            top_ref[...] = jnp.full(top_ref.shape, masked_score, F32)
            total_ref[...] = jnp.zeros(total_ref.shape, F32)
            mixed_ref[...] = jnp.zeros(mixed_ref.shape, F32)
            arrive([query_copy(role, dz) for dz in Z_HI])

            @pl.when(role == 0)
            def _():
                query_copy(0, 0).wait_recv()

        lane = lax.broadcasted_iota(jnp.int32, (1, tokens), 1)
        n = part * CHUNK + lane % (CHUNK * half) // half
        dz, move = route(n)
        source = (z + dz) % 2 * n_y + (y - sign * (1 - 2 * role) * move + n_y) % n_y
        limit = jnp.zeros_like(lane)
        for k in range(n_pool):
            holder = table_ref[k, row] >> 9
            limit = jnp.where(source == holder, length - (first_page + k) * page_tokens, limit)
        live = lane // (CHUNK * half) * half + lane % half < limit

        blocks = [
            jnp.concatenate([q_all[role, u, c] for u in range(QUARTERS)], axis=0)
            for c in range(BLOCKS)
        ]
        query = jnp.concatenate(blocks[:4], axis=1)
        rest = blocks[4][:, : LANES // 2]
        blank = jnp.zeros_like(rest)
        rest = jnp.concatenate(
            [jnp.concatenate([rest, blank], axis=1), jnp.concatenate([blank, rest], axis=1)], axis=0
        )
        first = part * CHUNK
        each(first, first + CHUNK - part, lambda n: page_copy(role, n).wait_recv())
        block = land[pl.ds(role * SITE + first, CHUNK)]

        def rows(begin):
            return block[:, begin : begin + half].reshape(CHUNK * half, LANES)

        keys = jnp.concatenate(
            [
                jnp.concatenate([rows(c * page_tokens + h * half) for c in range(4)], axis=1)
                for h in range(2)
            ],
            axis=0,
        )
        scores = lax.dot_general(query, keys, transposed, preferred_element_type=F32)
        extra = lax.dot_general(rest, rows(4 * page_tokens), transposed, preferred_element_type=F32)
        scores += jnp.concatenate([extra[:heads], extra[heads:]], axis=1)
        scores = jnp.where(live, scores * score_scale, masked_score)
        top = top_ref[...]
        new_top = jnp.maximum(top, jnp.max(scores, axis=1, keepdims=True))
        weights = jnp.where(live, jnp.exp(scores - new_top[:, :1]), 0.0)
        scale = jnp.exp(top - new_top)
        total = total_ref[...] * scale + jnp.sum(weights, axis=1, keepdims=True)
        update = jnp.dot(weights.astype(BF16), keys, preferred_element_type=F32)
        mixed = mixed_ref[...] * scale[:, :1] + update
        top_ref[...] = new_top
        total_ref[...] = total
        mixed_ref[...] = mixed

        @pl.when(step % 2 == 1)
        def _():
            some = total > 0.0
            safe = jnp.where(some, total, 1.0)
            inverse = 1.0 / safe
            even = mixed * inverse[:, :1]
            parts = split3(jnp.where(some, new_top + jnp.log(safe), masked_score))
            parts += (jnp.zeros_like(total),)
            for u, e in itertools.product(range(QUARTERS), range(2)):
                mine = slice(u * MSG + e * 8, u * MSG + e * 8 + 8)
                for c in range(4):
                    row = u * 8 * MSG + 2 * c + e
                    wide[pl.ds(row, 8, stride=MSG), :] = even[mine, c * LANES : (c + 1) * LANES]
                    wide[pl.ds(row + 8, 8, stride=MSG), :] = parts[c][mine]
            part_msg[role] = wide[: n_tp * MSG].astype(BF16).reshape(n_tp, MSG, LANES)
            start([part_copy(role, step) for step in TP])

            @pl.when(role == 0)
            def _():
                part_copy(0, SELF).start()

    each(0, 4, attend)
    part_land[1, tp] = part_msg[1, z_hi * 8 + here]
    part_copies = [part_copy(0, step) for step in TP + [SELF]]
    part_copies += [part_copy(1, step) for step in TP]
    arrive(part_copies)

    wide[...] = part_land[...].reshape(wide.shape).astype(F32)
    values = []
    for e in range(2):

        def rows(k, j):
            return wide[
                pl.ds(k // 4 * n_tp * MSG + k % 4 * MSG + 2 * j + e, GROUPS, stride=QUARTERS * MSG), :
            ]

        lses = [rows(k, 4) + rows(k, 5) + rows(k, 6) for k in range(2 * QUARTERS)]
        best = functools.reduce(jnp.maximum, lses)
        share = [jnp.exp(one - best) for one in lses]
        norm = 1.0 / functools.reduce(jnp.add, share)
        attended = []
        for c in range(4):
            block = functools.reduce(jnp.add, [share[k] * rows(k, c) for k in range(2 * QUARTERS)])
            attended.append((block * norm).astype(BF16))
        attended = jnp.concatenate(attended, axis=1)
        values.append(jnp.dot(attended, up_ref[e], preferred_element_type=F32))
    head_msg[...] = jnp.concatenate(values, axis=0).astype(BF16)

    def head_copy(step):
        return remote(
            head_msg, head_land.at[pool], (head_send, head_recv), number(step), to(tp, pool_of(step))
        )

    start(map(head_copy, POOL))
    head_land[pool] = head_msg[...]
    arrive(map(head_copy, POOL))

    landed = head_land[...].astype(F32)
    left = [landed[:, 8 * e : 8 * e + 8].reshape(4 * n_tp, LANES).astype(BF16) for e in range(2)]
    product = lax.dot_general(
        jnp.concatenate(left, axis=1), proj_ref[...], transposed, preferred_element_type=F32
    )
    columns = proj_ref.shape[0]
    blank = jnp.zeros((4 * n_tp, 4 * LANES - columns), F32)
    product = jnp.concatenate([product, blank], axis=1)
    for j in range(n_tp):
        last_msg[j] = product[4 * j : 4 * j + 4].astype(BF16)

    def last_copy(step):
        peer = tp_of(step)
        return remote(
            last_msg.at[peer], out_ref.at[tp], (last_send, last_recv), number(step), to(peer)
        )

    start(map(last_copy, TP))
    own = pltpu.make_async_copy(last_msg.at[tp], out_ref.at[tp], last_send.at[0])
    own.start()
    each(0, SITE - 1, lambda n: page_copy(0, n).wait_send())
    each(0, SITE - 1, lambda n: page_copy(1, n).wait_send())
    sent = [q_copy(step) for step in X_CORE]
    sent += [query_copy(0, dz) for dz in Z_HI + [0]] + [query_copy(1, dz) for dz in Z_HI]
    sent += part_copies
    sent += [head_copy(step) for step in POOL]
    sent += [last_copy(step) for step in TP]
    for copy in sent:
        copy.wait_send()
    own.wait()
    arrive(map(last_copy, TP))


def per_device(n_pool, n_tp, page_store, page_table, context_len, absorbed_query, value_up, out_proj):
    pages, tokens, key_width = page_store.shape
    requests = absorbed_query.shape[0]
    columns = out_proj.shape[1]
    hbm = pl.BlockSpec(memory_space=pltpu.HBM)
    message = lambda *lead: pltpu.VMEM((*lead, MSG, LANES), BF16)
    sems = lambda n: [pltpu.SemaphoreType.DMA((n,)), pltpu.SemaphoreType.DMA((n,))]
    summands = pl.pallas_call(
        functools.partial(kernel, n_pool, n_tp),
        out_shape=jax.ShapeDtypeStruct((n_tp, 4, 4 * LANES), BF16),
        in_specs=[hbm] * 6,
        out_specs=hbm,
        scratch_shapes=[
            pltpu.SMEM((n_pool, page_table.shape[0]), jnp.int32),
            pltpu.SMEM(context_len.shape, jnp.int32),
            pltpu.VMEM(page_store.shape, BF16),
            pltpu.VMEM(absorbed_query.shape, BF16),
            pltpu.VMEM(value_up.shape, BF16),
            pltpu.VMEM(out_proj.shape[::-1], BF16),
            pltpu.SemaphoreType.DMA((6,)),
            pltpu.VMEM((n_pool, tokens * key_width // LANES, LANES), BF16),
            pltpu.VMEM((n_pool, tokens * key_width // LANES, LANES), BF16),
            message(GROUPS),
            message(SITE, 2),
            message(2, BLOCKS),
            message(2, QUARTERS, BLOCKS),
            message(2, n_tp),
            message(2, n_tp),
            message(),
            message(n_pool),
            pltpu.VMEM((n_tp, 4, 4 * LANES), BF16),
            pltpu.VMEM((2 * n_tp * MSG, LANES), F32),
            pltpu.VMEM((2 * n_tp, LANES), F32),
            pltpu.VMEM((2 * n_tp, LANES), F32),
            pltpu.VMEM((2 * n_tp, value_up.shape[1]), F32),
            *sems(2 * SITE),
            *sems(4 * SITE),
            *sems(2 * QUARTERS),
            *sems(2 * n_tp),
            *sems(2 * SITE),
            *sems(n_tp),
        ],
        compiler_params=pltpu.CompilerParams(
            collective_id=0, has_side_effects=True, vmem_limit_bytes=62 * 1024 * 1024
        ),
        name="mla_decode",
    )(page_table.T, context_len, page_store, absorbed_query, value_up, out_proj.T)
    return jnp.sum(summands.astype(F32), axis=0)[:, :columns].astype(BF16)


def solution(mesh):
    placed = (
        P(("pool", "tp"), None, None),
        P(),
        P(),
        P("pool", "tp", None),
        P("tp", None, None),
        P("tp", "pool"),
    )
    return jax.shard_map(
        functools.partial(per_device, mesh.shape["pool"], mesh.shape["tp"]),
        mesh=mesh,
        in_specs=placed,
        out_specs=P("tp", "pool"),
        check_vma=False,
    )
```

```python
import functools
import itertools

import jax
import jax.numpy as jnp
from jax import lax
from jax.experimental import pallas as pl
from jax.experimental.pallas import tpu as pltpu
from jax.sharding import PartitionSpec as P

MESH = pl.DeviceIdType.MESH
score_scale = 192.0 ** (-0.5)
masked_score = -1e30
F32 = jnp.float32
BF16 = jnp.bfloat16
LANES = 128
MSG = 16
CHUNK = 4
FAR = 3
SITE = 8
X_CORE = [(2, 1), (2, 0), (1, 1), (3, 1), (1, 0), (3, 0), (0, 1)]
Z_HI = [2, 1, 3]
TP = [(dz, dx, dc) for dz in (2, 1, 3, 0) for dx in (2, 1, 3, 0) for dc in (1, 0)][:-1]
POOL = [(dz, dy) for dy in (4, 3, 5, 2, 6, 1, 7) for dz in (1, 0)] + [(1, 0)]
SITES = [(dz, dy) for dz, dy in POOL if dy not in (3, 4, 5)]
QUARTERS = 4
GROUPS = 8
BLOCKS = 5


def split3(x):
    hi = x.astype(BF16).astype(F32)
    mid = (x - hi).astype(BF16).astype(F32)
    return hi, mid, x - hi - mid


def each(first, last, body):
    def step(i, carry):
        body(i)
        return carry

    lax.fori_loop(first, last, step, 0)


def kernel(
    n_pool,
    n_tp,
    table_hbm,
    len_hbm,
    store_hbm,
    query_hbm,
    up_hbm,
    proj_hbm,
    out_ref,
    table_ref,
    len_ref,
    store_ref,
    query_ref,
    up_ref,
    proj_ref,
    local_sem,
    stage,
    land,
    q_msg,
    q_land,
    q_part,
    q_all,
    far_msg,
    far_land,
    part_msg,
    part_land,
    head_msg,
    head_land,
    last_msg,
    wide,
    page_send,
    page_recv,
    q_send,
    q_recv,
    all_send,
    all_recv,
    part_send,
    part_recv,
    head_send,
    head_recv,
    last_send,
    last_recv,
):
    pool = lax.axis_index("pool")
    tp = lax.axis_index("tp")
    n_y = n_pool // 2
    z, y = pool // n_y, pool % n_y
    sign = 1 - 2 * z
    page_tokens = store_ref.shape[1]
    requests = query_hbm.shape[0]
    request, quarter = tp // QUARTERS, tp % QUARTERS
    x, z_hi, core = tp // 8, tp // 2 % 4, tp % 2
    first_page = quarter * n_pool

    def place(at_z, at_y):
        return at_z * n_y + (at_y + 2 * n_y) % n_y

    def across(step):
        dx, dc = step
        return (x + dx) % 4 * 2 + (core + dc) % 2

    def along(dz):
        return (z_hi + dz) % 4

    def tp_of(step):
        dz, dx, dc = step
        return (x + dx) % 4 * 8 + (z_hi + dz) % 4 * 2 + (core + dc) % 2

    def pool_of(step):
        dz, dy = step
        return (z + dz) % 2 * n_y + (y + dy) % n_y

    def number(step):
        return step[0] * 8 + (step[1] if len(step) == 2 else step[1] * 2 + step[2])

    def to(tp_index, pool_index=pool):
        return {"pool": pool_index, "tp": tp_index}

    barrier = pltpu.get_barrier_semaphore()
    loads = [
        pltpu.make_async_copy(source, target, local_sem.at[i])
        for i, (source, target) in enumerate(
            [
                (table_hbm.at[pl.ds(pl.multiple_of(first_page, 8), n_pool)], table_ref),
                (store_hbm, store_ref),
                (query_hbm, query_ref),
                (len_hbm, len_ref),
                (up_hbm, up_ref),
                (proj_hbm, proj_ref),
            ]
        )
    ]
    for load in (loads[2], loads[0], loads[1]):
        load.start()

    def greet(tp_index, pool_index=pool):
        device = to(tp_index, pool_index)
        pl.semaphore_signal(barrier, inc=1, device_id=device, device_id_type=MESH)

    for step in X_CORE:
        greet(tp_of((0, *step)))
    for step in SITES:
        greet(tp, pool_of(step))
    for ahead in (FAR, -FAR):
        for dz in Z_HI + [0]:
            greet(tp_of((dz, 0, 0)), place(z, y + ahead))
    for dz in Z_HI:
        greet(tp_of((dz, 0, 0)))
    greetings = len(X_CORE) + len(SITES) + 2 * QUARTERS + len(Z_HI)
    for load in loads[3:]:
        load.start()

    me = pool * n_tp + tp

    def slot_of(group):
        row = group * requests + request

        def look(k, found):
            entry = table_ref[k, row]
            return found + jnp.where(entry >> 4 == me, entry & 15, 0)

        return lax.fori_loop(0, n_pool, look, 0, unroll=True)

    half = page_tokens // 2

    def packed(target, slot):
        for c in range(4):
            target[c * page_tokens : (c + 1) * page_tokens] = store_ref[
                slot, :, c * LANES : (c + 1) * LANES
            ]
        rest = store_ref[slot, :, 4 * LANES :]
        target[4 * page_tokens :] = jnp.concatenate([rest[:half], rest[half:]], axis=1)

    def remote(source, target, sems, i, device):
        send, recv = sems
        return pltpu.make_async_remote_copy(
            src_ref=source,
            dst_ref=target,
            send_sem=send.at[i],
            recv_sem=recv.at[i],
            device_id=device,
            device_id_type=MESH,
        )

    def start(copies):
        for copy in copies:
            copy.start()

    def arrive(copies):
        for copy in copies:
            copy.wait_recv()

    def route(n):
        k = n % 4
        return 1 - n // 4, (6 + k + n // 4 * (k // 2) * (6 * k - 11)) % n_y

    def page_copy(role, n):
        dz, move = route(n)
        to_z = (z + dz) % 2
        direction = (1 - 2 * to_z) * (1 - 2 * role)
        return remote(
            stage.at[role * SITE + n],
            land.at[role * SITE + n],
            (page_send, page_recv),
            role * SITE + n,
            to(tp, to_z * n_y + (y + direction * move + n_y) % n_y),
        )

    def send_pages(role, first, last):
        def send(i):
            n = (i + core * (SITE // 2)) % SITE
            dz, move = route(n)
            to_z = (z + dz) % 2
            direction = 1 - 2 * to_z
            ahead = direction * (1 - 2 * role) * move - direction * (1 - role) * FAR
            packed(stage.at[role * SITE + n], slot_of(to_z * n_y + (y + ahead + 2 * n_y) % n_y))

            @pl.when(n < SITE - 1)
            def _():
                page_copy(role, n).start()

        each(first, last, send)
        if last == SITE:
            local = role * SITE + SITE - 1
            land[local] = stage[local]

    loads[2].wait()
    for i in range(requests):
        for c in range(BLOCKS):
            width = min(LANES, query_ref.shape[-1] - c * LANES)
            wide[i * MSG + 2 * c : i * MSG + 2 * c + 2, :width] = query_ref[
                i, :, c * LANES : c * LANES + width
            ].astype(F32)
        wide[i * MSG + 2 * BLOCKS - 2 : (i + 1) * MSG, LANES // 2 :] = jnp.zeros((8, LANES // 2), F32)
        wide[i * MSG + 2 * BLOCKS : (i + 1) * MSG, : LANES // 2] = jnp.zeros((6, LANES // 2), F32)
    q_msg[...] = wide[: requests * MSG].astype(BF16).reshape(q_msg.shape)

    here = x * 2 + core

    def q_copy(step):
        peer = across(step)
        return remote(
            q_msg.at[pl.ds(peer // 2 * 2, 2)],
            q_land.at[here],
            (q_send, q_recv),
            number(step),
            to(tp_of((0, *step))),
        )

    pl.semaphore_wait(barrier, greetings)
    start(map(q_copy, X_CORE))
    loads[0].wait()
    loads[1].wait()
    send_pages(0, 0, SITE // 2)

    q_land[here] = q_msg[pl.ds(x * 2, 2)]
    arrive(map(q_copy, X_CORE))
    wide[: 2 * SITE * MSG] = q_land[...].reshape(2 * SITE * MSG, LANES).astype(F32)
    for i, c in itertools.product(range(2), range(BLOCKS)):
        halves = [wide[pl.ds(i * MSG + 2 * c + e, SITE, stride=2 * MSG), :] for e in range(2)]
        q_part[i, c] = jnp.concatenate(halves, axis=0).astype(BF16)

    def query_copy(role, dz):
        return remote(
            q_part.at[along(dz) // 2],
            q_all.at[role, z_hi],
            (all_send, all_recv),
            role * QUARTERS + dz,
            to(tp_of((dz, 0, 0)), z * n_y + (y + (1 - role) * sign * FAR + n_y) % n_y),
        )

    def part_copy(step):
        peer = tp_of(step)
        held = along(step[0]) * 8 + across(step[1:])
        return remote(
            part_msg.at[held], part_land.at[tp], (part_send, part_recv), number(step), to(peer)
        )

    def back_copy(rows=slice(None)):
        return remote(
            far_msg.at[rows], far_land.at[rows], (all_send, all_recv), 2 * QUARTERS, to(tp, place(z, y - sign * FAR))
        )

    start([query_copy(0, dz) for dz in Z_HI + [0]])
    start([query_copy(1, dz) for dz in Z_HI])
    q_all[1, z_hi] = q_part[z_hi // 2]
    send_pages(0, SITE // 2, SITE)
    send_pages(1, 0, SITE)
    for load in loads[3:]:
        load.wait()

    lat = up_ref.shape[1]
    heads = 2 * n_tp
    transposed = (((1,), (1,)), ((), ()))

    def attend(role, first, count, last, before):
        group = z * n_y + (y - sign * (1 - role) * FAR + n_y) % n_y
        row = group * requests + request
        length = len_ref[row]

        lane = lax.broadcasted_iota(jnp.int32, (1, count * page_tokens), 1)
        dz, move = route(first + lane % (count * half) // half)
        source = (z + dz) % 2 * n_y + (y - sign * (1 - 2 * role) * move + n_y) % n_y
        limit = jnp.zeros_like(lane)
        for k in range(n_pool):
            holder = table_ref[k, row] >> 9
            limit = jnp.where(source == holder, length - (first_page + k) * page_tokens, limit)
        live = lane // (count * half) * half + lane % half < limit

        each(first, last, lambda n: page_copy(role, n).wait_recv())
        if before is None:
            arrive([query_copy(role, dz) for dz in Z_HI + [0] * (1 - role)])
        blocks = [
            jnp.concatenate([q_all[role, u, c] for u in range(QUARTERS)], axis=0)
            for c in range(BLOCKS)
        ]
        query = jnp.concatenate(blocks[:4], axis=1)
        rest = blocks[4][:, : LANES // 2]
        blank = jnp.zeros_like(rest)
        rest = jnp.concatenate(
            [jnp.concatenate([rest, blank], axis=1), jnp.concatenate([blank, rest], axis=1)], axis=0
        )
        block = land[pl.ds(role * SITE + first, count)]

        def rows(begin):
            return block[:, begin : begin + half].reshape(count * half, LANES)

        keys = jnp.concatenate(
            [
                jnp.concatenate([rows(c * page_tokens + h * half) for c in range(4)], axis=1)
                for h in range(2)
            ],
            axis=0,
        )
        scores = lax.dot_general(query, keys, transposed, preferred_element_type=F32)
        extra = lax.dot_general(rest, rows(4 * page_tokens), transposed, preferred_element_type=F32)
        scores += jnp.concatenate([extra[:heads], extra[heads:]], axis=1)
        scores = jnp.where(live, scores * score_scale, masked_score)
        top = jnp.broadcast_to(jnp.max(scores, axis=1, keepdims=True), (heads, LANES))
        if before is not None:
            top = jnp.maximum(top, before[0])
        weights = jnp.where(live, jnp.exp(scores - top[:, :1]), 0.0)
        total = jnp.broadcast_to(jnp.sum(weights, axis=1, keepdims=True), (heads, LANES))
        mixed = jnp.dot(weights.astype(BF16), keys, preferred_element_type=F32)
        if before is not None:
            scale = jnp.exp(before[0] - top)
            total += before[1] * scale
            mixed += before[2] * scale[:, :1]
        return top, total, mixed

    def normalised(top, total, mixed):
        some = total > 0.0
        safe = jnp.where(some, total, 1.0)
        inverse = 1.0 / safe
        return jnp.where(some, top + jnp.log(safe), masked_score), mixed * inverse[:, :1]

    first, second = core * CHUNK, (1 - core) * CHUNK
    state = attend(0, first, CHUNK, first + CHUNK - core, None)
    lse, even = normalised(*attend(0, second, CHUNK, second + CHUNK - (1 - core), state))
    for c in range(4):
        far_msg[c * heads : (c + 1) * heads] = even[:, c * LANES : (c + 1) * LANES].astype(BF16)
    lane = lax.broadcasted_iota(jnp.int32, (heads, LANES), 1)
    hi, mid, low = split3(lse)
    stat = jnp.where(lane == 0, hi, jnp.where(lane == 1, mid, jnp.where(lane == 2, low, 0.0)))
    far_msg[4 * heads :] = stat.astype(BF16)
    start([back_copy(pl.ds(c * heads, heads)) for c in range(BLOCKS)])

    state = attend(1, first, CHUNK, first + CHUNK - core, None)
    top, total, mixed = attend(1, second, CHUNK, second + CHUNK - (1 - core), state)
    back_copy().wait_recv()
    back = jnp.sum(far_land[4 * heads :].astype(F32), axis=1, keepdims=True)
    new_top = jnp.maximum(top, back)
    scale = jnp.exp(top - new_top)
    share = jnp.where(back > 0.5 * masked_score, jnp.exp(back - new_top), 0.0)
    mixed = jnp.concatenate(
        [
            mixed[:, c * LANES : (c + 1) * LANES] * scale
            + far_land[c * heads : (c + 1) * heads].astype(F32) * share
            for c in range(4)
        ],
        axis=1,
    )
    lse, even = normalised(new_top, total * scale + share, mixed)
    parts = split3(lse) + (jnp.zeros_like(lse),)
    for u, e in itertools.product(range(QUARTERS), range(2)):
        mine = slice(u * MSG + e * 8, u * MSG + e * 8 + 8)
        for c in range(4):
            row = u * 8 * MSG + 2 * c + e
            wide[pl.ds(row, 8, stride=MSG), :] = even[mine, c * LANES : (c + 1) * LANES]
            wide[pl.ds(row + 8, 8, stride=MSG), :] = parts[c][mine]
    part_msg[...] = wide[...].astype(BF16).reshape(part_msg.shape)
    part_copies = [part_copy(step) for step in TP]
    start(part_copies)
    part_land[tp] = part_msg[z_hi * 8 + here]
    arrive(part_copies)

    wide[...] = part_land[...].reshape(wide.shape).astype(F32)
    values = []
    for e in range(2):

        def rows(k, j):
            return wide[pl.ds(k * MSG + 2 * j + e, GROUPS, stride=QUARTERS * MSG), :]

        lses = [rows(k, 4) + rows(k, 5) + rows(k, 6) for k in range(QUARTERS)]
        best = functools.reduce(jnp.maximum, lses)
        share = [jnp.exp(one - best) for one in lses]
        norm = 1.0 / functools.reduce(jnp.add, share)
        attended = []
        for c in range(4):
            block = functools.reduce(jnp.add, [share[k] * rows(k, c) for k in range(QUARTERS)])
            attended.append((block * norm).astype(BF16))
        attended = jnp.concatenate(attended, axis=1)
        values.append(jnp.dot(attended, up_ref[e], preferred_element_type=F32))
    head_msg[...] = jnp.concatenate(values, axis=0).astype(BF16)

    def head_copy(step):
        return remote(
            head_msg, head_land.at[pool], (head_send, head_recv), number(step), to(tp, pool_of(step))
        )

    start(map(head_copy, POOL))
    head_land[pool] = head_msg[...]
    arrive(map(head_copy, POOL))

    landed = head_land[...].astype(F32)
    left = [landed[:, 8 * e : 8 * e + 8].reshape(4 * n_tp, LANES).astype(BF16) for e in range(2)]
    product = lax.dot_general(
        jnp.concatenate(left, axis=1), proj_ref[...], transposed, preferred_element_type=F32
    )
    columns = proj_ref.shape[0]
    blank = jnp.zeros((4 * n_tp, 4 * LANES - columns), F32)
    product = jnp.concatenate([product, blank], axis=1)
    for j in range(n_tp):
        last_msg[j] = product[4 * j : 4 * j + 4].astype(BF16)

    def last_copy(step):
        peer = tp_of(step)
        return remote(
            last_msg.at[peer], out_ref.at[tp], (last_send, last_recv), number(step), to(peer)
        )

    start(map(last_copy, TP))
    own = pltpu.make_async_copy(last_msg.at[tp], out_ref.at[tp], last_send.at[0])
    own.start()
    each(0, SITE - 1, lambda n: page_copy(0, n).wait_send())
    each(0, SITE - 1, lambda n: page_copy(1, n).wait_send())
    sent = [q_copy(step) for step in X_CORE]
    sent += [query_copy(0, dz) for dz in Z_HI + [0]] + [query_copy(1, dz) for dz in Z_HI]
    sent += [back_copy()] + part_copies
    sent += [head_copy(step) for step in POOL]
    sent += [last_copy(step) for step in TP]
    for copy in sent:
        copy.wait_send()
    own.wait()
    arrive(map(last_copy, TP))


def per_device(n_pool, n_tp, page_store, page_table, context_len, absorbed_query, value_up, out_proj):
    pages, tokens, key_width = page_store.shape
    requests = absorbed_query.shape[0]
    columns = out_proj.shape[1]
    hbm = pl.BlockSpec(memory_space=pltpu.HBM)
    message = lambda *lead: pltpu.VMEM((*lead, MSG, LANES), BF16)
    sems = lambda n: [pltpu.SemaphoreType.DMA((n,)), pltpu.SemaphoreType.DMA((n,))]
    summands = pl.pallas_call(
        functools.partial(kernel, n_pool, n_tp),
        out_shape=jax.ShapeDtypeStruct((n_tp, 4, 4 * LANES), BF16),
        in_specs=[hbm] * 6,
        out_specs=hbm,
        scratch_shapes=[
            pltpu.SMEM((n_pool, page_table.shape[0]), jnp.int32),
            pltpu.SMEM(context_len.shape, jnp.int32),
            pltpu.VMEM(page_store.shape, BF16),
            pltpu.VMEM(absorbed_query.shape, BF16),
            pltpu.VMEM(value_up.shape, BF16),
            pltpu.VMEM(out_proj.shape[::-1], BF16),
            pltpu.SemaphoreType.DMA((6,)),
            pltpu.VMEM((n_pool, tokens * key_width // LANES, LANES), BF16),
            pltpu.VMEM((n_pool, tokens * key_width // LANES, LANES), BF16),
            message(GROUPS),
            message(SITE, 2),
            message(2, BLOCKS),
            message(2, QUARTERS, BLOCKS),
            pltpu.VMEM((BLOCKS * 2 * n_tp, LANES), BF16),
            pltpu.VMEM((BLOCKS * 2 * n_tp, LANES), BF16),
            message(n_tp),
            message(n_tp),
            message(),
            message(n_pool),
            pltpu.VMEM((n_tp, 4, 4 * LANES), BF16),
            pltpu.VMEM((n_tp * MSG, LANES), F32),
            *sems(2 * SITE),
            *sems(4 * SITE),
            *sems(2 * QUARTERS + 1),
            *sems(n_tp),
            *sems(2 * SITE),
            *sems(n_tp),
        ],
        compiler_params=pltpu.CompilerParams(
            collective_id=0, has_side_effects=True, vmem_limit_bytes=62 * 1024 * 1024
        ),
        name="mla_decode",
    )(page_table.T, context_len, page_store, absorbed_query, value_up, out_proj.T)
    return jnp.sum(summands.astype(F32), axis=0)[:, :columns].astype(BF16)


def solution(mesh):
    placed = (
        P(("pool", "tp"), None, None),
        P(),
        P(),
        P("pool", "tp", None),
        P("tp", None, None),
        P("tp", "pool"),
    )
    return jax.shard_map(
        functools.partial(per_device, mesh.shape["pool"], mesh.shape["tp"]),
        mesh=mesh,
        in_specs=placed,
        out_specs=P("tp", "pool"),
        check_vma=False,
    )
```

```python
import functools
import itertools

import jax
import jax.numpy as jnp
from jax import lax
from jax.experimental import pallas as pl
from jax.experimental.pallas import tpu as pltpu
from jax.sharding import PartitionSpec as P

MESH = pl.DeviceIdType.MESH
score_scale = 192.0 ** (-0.5)
masked_score = -1e30
F32 = jnp.float32
BF16 = jnp.bfloat16
LANES = 128
MSG = 16
CHUNK = 4
FAR = 3
SITE = 8
X_CORE = [(2, 1), (2, 0), (1, 1), (3, 1), (1, 0), (3, 0), (0, 1)]
Z_HI = [2, 1, 3]
TP = [(dz, dx, dc) for dz in (2, 1, 3, 0) for dx in (2, 1, 3, 0) for dc in (1, 0)][:-1]
POOL = [(dz, dy) for dy in (4, 3, 5, 2, 6, 1, 7) for dz in (1, 0)] + [(1, 0)]
SITES = [(dz, dy) for dz, dy in POOL if dy not in (3, 4, 5)]
QUARTERS = 4
GROUPS = 8
BLOCKS = 5


def split3(x):
    hi = x.astype(BF16).astype(F32)
    mid = (x - hi).astype(BF16).astype(F32)
    return hi, mid, x - hi - mid


def each(first, last, body):
    def step(i, carry):
        body(i)
        return carry

    lax.fori_loop(first, last, step, 0)


def kernel(
    n_pool,
    n_tp,
    table_hbm,
    len_hbm,
    store_hbm,
    query_hbm,
    up_hbm,
    proj_hbm,
    out_ref,
    table_ref,
    len_ref,
    store_ref,
    query_ref,
    up_ref,
    proj_ref,
    local_sem,
    stage,
    land,
    q_msg,
    q_land,
    q_part,
    q_all,
    far_msg,
    far_land,
    part_msg,
    part_land,
    head_msg,
    head_land,
    last_msg,
    wide,
    page_send,
    page_recv,
    q_send,
    q_recv,
    all_send,
    all_recv,
    part_send,
    part_recv,
    head_send,
    head_recv,
    last_send,
    last_recv,
):
    pool = lax.axis_index("pool")
    tp = lax.axis_index("tp")
    n_y = n_pool // 2
    z, y = pool // n_y, pool % n_y
    sign = 1 - 2 * z
    page_tokens = store_ref.shape[1]
    requests = query_hbm.shape[0]
    request, quarter = tp // QUARTERS, tp % QUARTERS
    x, z_hi, core = tp // 8, tp // 2 % 4, tp % 2
    first_page = quarter * n_pool

    def place(at_z, at_y):
        return at_z * n_y + (at_y + 2 * n_y) % n_y

    def across(step):
        dx, dc = step
        return (x + dx) % 4 * 2 + (core + dc) % 2

    def along(dz):
        return (z_hi + dz) % 4

    def tp_of(step):
        dz, dx, dc = step
        return (x + dx) % 4 * 8 + (z_hi + dz) % 4 * 2 + (core + dc) % 2

    def pool_of(step):
        dz, dy = step
        return (z + dz) % 2 * n_y + (y + dy) % n_y

    def number(step):
        return step[0] * 8 + (step[1] if len(step) == 2 else step[1] * 2 + step[2])

    def to(tp_index, pool_index=pool):
        return {"pool": pool_index, "tp": tp_index}

    barrier = pltpu.get_barrier_semaphore()
    loads = [
        pltpu.make_async_copy(source, target, local_sem.at[i])
        for i, (source, target) in enumerate(
            [
                (table_hbm.at[pl.ds(pl.multiple_of(first_page, 8), n_pool)], table_ref),
                (store_hbm, store_ref),
                (query_hbm, query_ref),
                (len_hbm, len_ref),
                (up_hbm, up_ref),
                (proj_hbm, proj_ref),
            ]
        )
    ]
    for load in (loads[2], loads[0], loads[1]):
        load.start()

    def greet(tp_index, pool_index=pool):
        device = to(tp_index, pool_index)
        pl.semaphore_signal(barrier, inc=1, device_id=device, device_id_type=MESH)

    for step in X_CORE:
        greet(tp_of((0, *step)))
    for step in SITES:
        greet(tp, pool_of(step))
    for ahead in (FAR, -FAR):
        for dz in Z_HI + [0]:
            greet(tp_of((dz, 0, 0)), place(z, y + ahead))
    for dz in Z_HI:
        greet(tp_of((dz, 0, 0)))
    greetings = len(X_CORE) + len(SITES) + 2 * QUARTERS + len(Z_HI)
    for load in loads[3:]:
        load.start()

    me = pool * n_tp + tp

    def slot_of(group):
        row = group * requests + request

        def look(k, found):
            entry = table_ref[k, row]
            return found + jnp.where(entry >> 4 == me, entry & 15, 0)

        return lax.fori_loop(0, n_pool, look, 0, unroll=True)

    half = page_tokens // 2

    def packed(target, slot):
        for c in range(4):
            target[c * page_tokens : (c + 1) * page_tokens] = store_ref[
                slot, :, c * LANES : (c + 1) * LANES
            ]
        rest = store_ref[slot, :, 4 * LANES :]
        target[4 * page_tokens :] = jnp.concatenate([rest[:half], rest[half:]], axis=1)

    def remote(source, target, sems, i, device):
        send, recv = sems
        return pltpu.make_async_remote_copy(
            src_ref=source,
            dst_ref=target,
            send_sem=send.at[i],
            recv_sem=recv.at[i],
            device_id=device,
            device_id_type=MESH,
        )

    def start(copies):
        for copy in copies:
            copy.start()

    def arrive(copies):
        for copy in copies:
            copy.wait_recv()

    def route(n):
        k = n % 4
        return 1 - n // 4, (6 + k + n // 4 * (k // 2) * (6 * k - 11)) % n_y

    def page_copy(role, n):
        dz, move = route(n)
        to_z = (z + dz) % 2
        direction = (1 - 2 * to_z) * (1 - 2 * role)
        return remote(
            stage.at[role * SITE + n],
            land.at[role * SITE + n],
            (page_send, page_recv),
            role * SITE + n,
            to(tp, to_z * n_y + (y + direction * move + n_y) % n_y),
        )

    def page_in_turn(i):
        return (i + core * (SITE // 2)) % SITE

    def pack_page(role, i):
        n = page_in_turn(i)
        dz, move = route(n)
        to_z = (z + dz) % 2
        direction = 1 - 2 * to_z
        ahead = direction * (1 - 2 * role) * move - direction * (1 - role) * FAR
        packed(stage.at[role * SITE + n], slot_of(to_z * n_y + (y + ahead + 2 * n_y) % n_y))

    def send_page(role, i):
        n = page_in_turn(i)

        @pl.when(n < SITE - 1)
        def _():
            page_copy(role, n).start()

    def pack_and_send(i):
        pack_page(0, i)
        send_page(0, i)

    loads[2].wait()
    for i in range(requests):
        for c in range(BLOCKS):
            width = min(LANES, query_ref.shape[-1] - c * LANES)
            wide[i * MSG + 2 * c : i * MSG + 2 * c + 2, :width] = query_ref[
                i, :, c * LANES : c * LANES + width
            ].astype(F32)
        wide[i * MSG + 2 * BLOCKS - 2 : (i + 1) * MSG, LANES // 2 :] = jnp.zeros((8, LANES // 2), F32)
        wide[i * MSG + 2 * BLOCKS : (i + 1) * MSG, : LANES // 2] = jnp.zeros((6, LANES // 2), F32)
    q_msg[...] = wide[: requests * MSG].astype(BF16).reshape(q_msg.shape)

    here = x * 2 + core

    def q_copy(step):
        peer = across(step)
        return remote(
            q_msg.at[pl.ds(peer // 2 * 2, 2)],
            q_land.at[here],
            (q_send, q_recv),
            number(step),
            to(tp_of((0, *step))),
        )

    pl.semaphore_wait(barrier, greetings)
    start(map(q_copy, X_CORE))
    loads[0].wait()
    loads[1].wait()
    each(0, SITE // 2, pack_and_send)
    each(SITE // 2, SITE, lambda i: pack_page(0, i))
    each(0, SITE, lambda i: pack_page(1, i))
    for role in range(2):
        land[role * SITE + SITE - 1] = stage[role * SITE + SITE - 1]

    q_land[here] = q_msg[pl.ds(x * 2, 2)]
    arrive(map(q_copy, X_CORE))
    wide[: 2 * SITE * MSG] = q_land[...].reshape(2 * SITE * MSG, LANES).astype(F32)
    for i, c in itertools.product(range(2), range(BLOCKS)):
        halves = [wide[pl.ds(i * MSG + 2 * c + e, SITE, stride=2 * MSG), :] for e in range(2)]
        q_part[i, c] = jnp.concatenate(halves, axis=0).astype(BF16)

    def query_copy(role, dz):
        return remote(
            q_part.at[along(dz) // 2],
            q_all.at[role, z_hi],
            (all_send, all_recv),
            role * QUARTERS + dz,
            to(tp_of((dz, 0, 0)), z * n_y + (y + (1 - role) * sign * FAR + n_y) % n_y),
        )

    def part_copy(step):
        peer = tp_of(step)
        held = along(step[0]) * 8 + across(step[1:])
        return remote(
            part_msg.at[held], part_land.at[tp], (part_send, part_recv), number(step), to(peer)
        )

    def back_copy(rows=slice(None)):
        return remote(
            far_msg.at[rows], far_land.at[rows], (all_send, all_recv), 2 * QUARTERS, to(tp, place(z, y - sign * FAR))
        )

    start([query_copy(0, dz) for dz in Z_HI + [0]])
    start([query_copy(1, dz) for dz in Z_HI])
    q_all[1, z_hi] = q_part[z_hi // 2]
    each(SITE // 2, SITE, lambda i: send_page(0, i))
    each(0, SITE, lambda i: send_page(1, i))
    for load in loads[3:]:
        load.wait()

    lat = up_ref.shape[1]
    heads = 2 * n_tp
    transposed = (((1,), (1,)), ((), ()))

    def attend(role, first, count, last, before):
        group = z * n_y + (y - sign * (1 - role) * FAR + n_y) % n_y
        row = group * requests + request
        length = len_ref[row]

        lane = lax.broadcasted_iota(jnp.int32, (1, count * page_tokens), 1)
        dz, move = route(first + lane % (count * half) // half)
        source = (z + dz) % 2 * n_y + (y - sign * (1 - 2 * role) * move + n_y) % n_y
        limit = jnp.zeros_like(lane)
        for k in range(n_pool):
            holder = table_ref[k, row] >> 9
            limit = jnp.where(source == holder, length - (first_page + k) * page_tokens, limit)
        live = lane // (count * half) * half + lane % half < limit

        each(first, last, lambda n: page_copy(role, n).wait_recv())
        if before is None:
            arrive([query_copy(role, dz) for dz in Z_HI + [0] * (1 - role)])
        blocks = [
            jnp.concatenate([q_all[role, u, c] for u in range(QUARTERS)], axis=0)
            for c in range(BLOCKS)
        ]
        query = jnp.concatenate(blocks[:4], axis=1)
        rest = blocks[4][:, : LANES // 2]
        blank = jnp.zeros_like(rest)
        rest = jnp.concatenate(
            [jnp.concatenate([rest, blank], axis=1), jnp.concatenate([blank, rest], axis=1)], axis=0
        )
        block = land[pl.ds(role * SITE + first, count)]

        def rows(begin):
            return block[:, begin : begin + half].reshape(count * half, LANES)

        keys = jnp.concatenate(
            [
                jnp.concatenate([rows(c * page_tokens + h * half) for c in range(4)], axis=1)
                for h in range(2)
            ],
            axis=0,
        )
        scores = lax.dot_general(query, keys, transposed, preferred_element_type=F32)
        extra = lax.dot_general(rest, rows(4 * page_tokens), transposed, preferred_element_type=F32)
        scores += jnp.concatenate([extra[:heads], extra[heads:]], axis=1)
        scores = jnp.where(live, scores * score_scale, masked_score)
        top = jnp.broadcast_to(jnp.max(scores, axis=1, keepdims=True), (heads, LANES))
        if before is not None:
            top = jnp.maximum(top, before[0])
        weights = jnp.where(live, jnp.exp(scores - top[:, :1]), 0.0)
        total = jnp.broadcast_to(jnp.sum(weights, axis=1, keepdims=True), (heads, LANES))
        mixed = jnp.dot(weights.astype(BF16), keys, preferred_element_type=F32)
        if before is not None:
            scale = jnp.exp(before[0] - top)
            total += before[1] * scale
            mixed += before[2] * scale[:, :1]
        return top, total, mixed

    def normalised(top, total, mixed):
        some = total > 0.0
        safe = jnp.where(some, total, 1.0)
        inverse = 1.0 / safe
        return jnp.where(some, top + jnp.log(safe), masked_score), mixed * inverse[:, :1]

    first, second = core * CHUNK, (1 - core) * CHUNK
    state = attend(0, first, CHUNK, first + CHUNK - core, None)
    lse, even = normalised(*attend(0, second, CHUNK, second + CHUNK - (1 - core), state))
    for c in range(4):
        far_msg[c * heads : (c + 1) * heads] = even[:, c * LANES : (c + 1) * LANES].astype(BF16)
    lane = lax.broadcasted_iota(jnp.int32, (heads, LANES), 1)
    hi, mid, low = split3(lse)
    stat = jnp.where(lane == 0, hi, jnp.where(lane == 1, mid, jnp.where(lane == 2, low, 0.0)))
    far_msg[4 * heads :] = stat.astype(BF16)
    start([back_copy(pl.ds(c * heads, heads)) for c in range(BLOCKS)])

    state = attend(1, first, CHUNK, first + CHUNK - core, None)
    top, total, mixed = attend(1, second, CHUNK, second + CHUNK - (1 - core), state)
    back_copy().wait_recv()
    back = jnp.sum(far_land[4 * heads :].astype(F32), axis=1, keepdims=True)
    new_top = jnp.maximum(top, back)
    scale = jnp.exp(top - new_top)
    share = jnp.where(back > 0.5 * masked_score, jnp.exp(back - new_top), 0.0)
    mixed = jnp.concatenate(
        [
            mixed[:, c * LANES : (c + 1) * LANES] * scale
            + far_land[c * heads : (c + 1) * heads].astype(F32) * share
            for c in range(4)
        ],
        axis=1,
    )
    lse, even = normalised(new_top, total * scale + share, mixed)
    parts = split3(lse) + (jnp.zeros_like(lse),)
    for u, e in itertools.product(range(QUARTERS), range(2)):
        mine = slice(u * MSG + e * 8, u * MSG + e * 8 + 8)
        for c in range(4):
            row = u * 8 * MSG + 2 * c + e
            wide[pl.ds(row, 8, stride=MSG), :] = even[mine, c * LANES : (c + 1) * LANES]
            wide[pl.ds(row + 8, 8, stride=MSG), :] = parts[c][mine]
    part_msg[...] = wide[...].astype(BF16).reshape(part_msg.shape)
    part_copies = [part_copy(step) for step in TP]
    start(part_copies)
    part_land[tp] = part_msg[z_hi * 8 + here]
    arrive(part_copies)

    wide[...] = part_land[...].reshape(wide.shape).astype(F32)
    values = []
    for e in range(2):

        def rows(k, j):
            return wide[pl.ds(k * MSG + 2 * j + e, GROUPS, stride=QUARTERS * MSG), :]

        lses = [rows(k, 4) + rows(k, 5) + rows(k, 6) for k in range(QUARTERS)]
        best = functools.reduce(jnp.maximum, lses)
        share = [jnp.exp(one - best) for one in lses]
        norm = 1.0 / functools.reduce(jnp.add, share)
        attended = []
        for c in range(4):
            block = functools.reduce(jnp.add, [share[k] * rows(k, c) for k in range(QUARTERS)])
            attended.append((block * norm).astype(BF16))
        attended = jnp.concatenate(attended, axis=1)
        values.append(jnp.dot(attended, up_ref[e], preferred_element_type=F32))
    head_msg[...] = jnp.concatenate(values, axis=0).astype(BF16)

    def head_copy(step):
        return remote(
            head_msg, head_land.at[pool], (head_send, head_recv), number(step), to(tp, pool_of(step))
        )

    start(map(head_copy, POOL))
    head_land[pool] = head_msg[...]
    arrive(map(head_copy, POOL))

    landed = head_land[...].astype(F32)
    left = [landed[:, 8 * e : 8 * e + 8].reshape(4 * n_tp, LANES).astype(BF16) for e in range(2)]
    product = lax.dot_general(
        jnp.concatenate(left, axis=1), proj_ref[...], transposed, preferred_element_type=F32
    )
    columns = proj_ref.shape[0]
    blank = jnp.zeros((4 * n_tp, 4 * LANES - columns), F32)
    product = jnp.concatenate([product, blank], axis=1)
    for j in range(n_tp):
        last_msg[j] = product[4 * j : 4 * j + 4].astype(BF16)

    def last_copy(step):
        peer = tp_of(step)
        return remote(
            last_msg.at[peer], out_ref.at[tp], (last_send, last_recv), number(step), to(peer)
        )

    start(map(last_copy, TP))
    own = pltpu.make_async_copy(last_msg.at[tp], out_ref.at[tp], last_send.at[0])
    own.start()
    each(0, SITE - 1, lambda n: page_copy(0, n).wait_send())
    each(0, SITE - 1, lambda n: page_copy(1, n).wait_send())
    sent = [q_copy(step) for step in X_CORE]
    sent += [query_copy(0, dz) for dz in Z_HI + [0]] + [query_copy(1, dz) for dz in Z_HI]
    sent += [back_copy()] + part_copies
    sent += [head_copy(step) for step in POOL]
    sent += [last_copy(step) for step in TP]
    for copy in sent:
        copy.wait_send()
    own.wait()
    arrive(map(last_copy, TP))


def per_device(n_pool, n_tp, page_store, page_table, context_len, absorbed_query, value_up, out_proj):
    pages, tokens, key_width = page_store.shape
    requests = absorbed_query.shape[0]
    columns = out_proj.shape[1]
    hbm = pl.BlockSpec(memory_space=pltpu.HBM)
    message = lambda *lead: pltpu.VMEM((*lead, MSG, LANES), BF16)
    sems = lambda n: [pltpu.SemaphoreType.DMA((n,)), pltpu.SemaphoreType.DMA((n,))]
    summands = pl.pallas_call(
        functools.partial(kernel, n_pool, n_tp),
        out_shape=jax.ShapeDtypeStruct((n_tp, 4, 4 * LANES), BF16),
        in_specs=[hbm] * 6,
        out_specs=hbm,
        scratch_shapes=[
            pltpu.SMEM((n_pool, page_table.shape[0]), jnp.int32),
            pltpu.SMEM(context_len.shape, jnp.int32),
            pltpu.VMEM(page_store.shape, BF16),
            pltpu.VMEM(absorbed_query.shape, BF16),
            pltpu.VMEM(value_up.shape, BF16),
            pltpu.VMEM(out_proj.shape[::-1], BF16),
            pltpu.SemaphoreType.DMA((6,)),
            pltpu.VMEM((n_pool, tokens * key_width // LANES, LANES), BF16),
            pltpu.VMEM((n_pool, tokens * key_width // LANES, LANES), BF16),
            message(GROUPS),
            message(SITE, 2),
            message(2, BLOCKS),
            message(2, QUARTERS, BLOCKS),
            pltpu.VMEM((BLOCKS * 2 * n_tp, LANES), BF16),
            pltpu.VMEM((BLOCKS * 2 * n_tp, LANES), BF16),
            message(n_tp),
            message(n_tp),
            message(),
            message(n_pool),
            pltpu.VMEM((n_tp, 4, 4 * LANES), BF16),
            pltpu.VMEM((n_tp * MSG, LANES), F32),
            *sems(2 * SITE),
            *sems(4 * SITE),
            *sems(2 * QUARTERS + 1),
            *sems(n_tp),
            *sems(2 * SITE),
            *sems(n_tp),
        ],
        compiler_params=pltpu.CompilerParams(
            collective_id=0, has_side_effects=True, vmem_limit_bytes=62 * 1024 * 1024
        ),
        name="mla_decode",
    )(page_table.T, context_len, page_store, absorbed_query, value_up, out_proj.T)
    return jnp.sum(summands.astype(F32), axis=0)[:, :columns].astype(BF16)


def solution(mesh):
    placed = (
        P(("pool", "tp"), None, None),
        P(),
        P(),
        P("pool", "tp", None),
        P("tp", None, None),
        P("tp", "pool"),
    )
    return jax.shard_map(
        functools.partial(per_device, mesh.shape["pool"], mesh.shape["tp"]),
        mesh=mesh,
        in_specs=placed,
        out_specs=P("tp", "pool"),
        check_vma=False,
    )
```

```python
import functools
import itertools

import jax
import jax.numpy as jnp
from jax import lax
from jax.experimental import pallas as pl
from jax.experimental.pallas import tpu as pltpu
from jax.sharding import PartitionSpec as P

MESH = pl.DeviceIdType.MESH
score_scale = 192.0 ** (-0.5)
masked_score = -1e30
F32 = jnp.float32
BF16 = jnp.bfloat16
LANES = 128
MSG = 16
CHUNK = 4
FAR = 3
SITE = 8
X_CORE = [(2, 1), (2, 0), (1, 1), (3, 1), (1, 0), (3, 0), (0, 1)]
Z_HI = [2, 1, 3]
TP = [(dz, dx, dc) for dz in (2, 1, 3, 0) for dx in (2, 1, 3, 0) for dc in (1, 0)][:-1]
POOL = [(dz, dy) for dy in (4, 3, 5, 2, 6, 1, 7) for dz in (1, 0)] + [(1, 0)]
SITES = [(dz, dy) for dz, dy in POOL if dy not in (3, 4, 5)]
QUARTERS = 4
GROUPS = 8
BLOCKS = 5


def split3(x):
    hi = x.astype(BF16).astype(F32)
    mid = (x - hi).astype(BF16).astype(F32)
    return hi, mid, x - hi - mid


def each(first, last, body):
    def step(i, carry):
        body(i)
        return carry

    lax.fori_loop(first, last, step, 0)


def kernel(
    n_pool,
    n_tp,
    table_hbm,
    len_hbm,
    store_hbm,
    query_hbm,
    up_hbm,
    proj_hbm,
    out_ref,
    near_hbm,
    table_ref,
    len_ref,
    store_ref,
    query_ref,
    up_ref,
    proj_ref,
    local_sem,
    near_sem,
    stage,
    land,
    q_msg,
    q_land,
    q_part,
    q_all,
    far_msg,
    far_land,
    part_msg,
    part_land,
    head_msg,
    head_land,
    last_msg,
    wide,
    page_send,
    page_recv,
    q_send,
    q_recv,
    all_send,
    all_recv,
    part_send,
    part_recv,
    head_send,
    head_recv,
    last_send,
    last_recv,
):
    pool = lax.axis_index("pool")
    tp = lax.axis_index("tp")
    n_y = n_pool // 2
    z, y = pool // n_y, pool % n_y
    sign = 1 - 2 * z
    page_tokens = store_ref.shape[1]
    requests = query_hbm.shape[0]
    request, quarter = tp // QUARTERS, tp % QUARTERS
    x, z_hi, core = tp // 8, tp // 2 % 4, tp % 2
    first_page = quarter * n_pool

    def place(at_z, at_y):
        return at_z * n_y + (at_y + 2 * n_y) % n_y

    def across(step):
        dx, dc = step
        return (x + dx) % 4 * 2 + (core + dc) % 2

    def along(dz):
        return (z_hi + dz) % 4

    def tp_of(step):
        dz, dx, dc = step
        return (x + dx) % 4 * 8 + (z_hi + dz) % 4 * 2 + (core + dc) % 2

    def pool_of(step):
        dz, dy = step
        return (z + dz) % 2 * n_y + (y + dy) % n_y

    def number(step):
        return step[0] * 8 + (step[1] if len(step) == 2 else step[1] * 2 + step[2])

    def to(tp_index, pool_index=pool):
        return {"pool": pool_index, "tp": tp_index}

    barrier = pltpu.get_barrier_semaphore()
    loads = [
        pltpu.make_async_copy(source, target, local_sem.at[i])
        for i, (source, target) in enumerate(
            [
                (table_hbm.at[pl.ds(pl.multiple_of(first_page, 8), n_pool)], table_ref),
                (store_hbm, store_ref),
                (query_hbm, query_ref),
                (len_hbm, len_ref),
                (up_hbm, up_ref),
                (proj_hbm, proj_ref),
            ]
        )
    ]
    for load in (loads[2], loads[0], loads[1]):
        load.start()

    def greet(tp_index, pool_index=pool):
        device = to(tp_index, pool_index)
        pl.semaphore_signal(barrier, inc=1, device_id=device, device_id_type=MESH)

    for step in X_CORE:
        greet(tp_of((0, *step)))
    for step in SITES:
        greet(tp, pool_of(step))
    for ahead in (FAR, -FAR):
        for dz in Z_HI + [0]:
            greet(tp_of((dz, 0, 0)), place(z, y + ahead))
    for dz in Z_HI:
        greet(tp_of((dz, 0, 0)))
    greetings = len(X_CORE) + len(SITES) + 2 * QUARTERS + len(Z_HI)
    for load in loads[3:]:
        load.start()

    me = pool * n_tp + tp

    def slot_of(group):
        row = group * requests + request

        def look(k, found):
            entry = table_ref[k, row]
            return found + jnp.where(entry >> 4 == me, entry & 15, 0)

        return lax.fori_loop(0, n_pool, look, 0, unroll=True)

    half = page_tokens // 2

    def packed(target, slot):
        for c in range(4):
            target[c * page_tokens : (c + 1) * page_tokens] = store_ref[
                slot, :, c * LANES : (c + 1) * LANES
            ]
        rest = store_ref[slot, :, 4 * LANES :]
        target[4 * page_tokens :] = jnp.concatenate([rest[:half], rest[half:]], axis=1)

    def remote(source, target, sems, i, device):
        send, recv = sems
        return pltpu.make_async_remote_copy(
            src_ref=source,
            dst_ref=target,
            send_sem=send.at[i],
            recv_sem=recv.at[i],
            device_id=device,
            device_id_type=MESH,
        )

    def start(copies):
        for copy in copies:
            copy.start()

    def arrive(copies):
        for copy in copies:
            copy.wait_recv()

    def route(n):
        k = n % 4
        return 1 - n // 4, (6 + k + n // 4 * (k // 2) * (6 * k - 11)) % n_y

    def page_copy(role, n):
        dz, move = route(n)
        to_z = (z + dz) % 2
        direction = (1 - 2 * to_z) * (1 - 2 * role)
        source = near_hbm.at[n] if isinstance(role, int) and role == 1 else stage.at[n]
        return remote(
            source,
            land.at[role * SITE + n],
            (page_send, page_recv),
            role * SITE + n,
            to(tp, to_z * n_y + (y + direction * move + n_y) % n_y),
        )

    def page_in_turn(i):
        return (i + core * (SITE // 2)) % SITE

    def pack_page(role, i):
        n = page_in_turn(i)
        dz, move = route(n)
        to_z = (z + dz) % 2
        direction = 1 - 2 * to_z
        ahead = direction * (1 - 2 * role) * move - direction * (1 - role) * FAR
        packed(stage.at[role * SITE + n], slot_of(to_z * n_y + (y + ahead + 2 * n_y) % n_y))

    def send_page(role, i):
        n = page_in_turn(i)

        @pl.when(n < SITE - 1)
        def _():
            page_copy(role, n).start()

    def pack_and_send(i):
        pack_page(0, i)
        send_page(0, i)

    loads[2].wait()
    for i in range(requests):
        for c in range(BLOCKS):
            width = min(LANES, query_ref.shape[-1] - c * LANES)
            wide[i * MSG + 2 * c : i * MSG + 2 * c + 2, :width] = query_ref[
                i, :, c * LANES : c * LANES + width
            ].astype(F32)
        wide[i * MSG + 2 * BLOCKS - 2 : (i + 1) * MSG, LANES // 2 :] = jnp.zeros((8, LANES // 2), F32)
        wide[i * MSG + 2 * BLOCKS : (i + 1) * MSG, : LANES // 2] = jnp.zeros((6, LANES // 2), F32)
    q_msg[...] = wide[: requests * MSG].astype(BF16).reshape(q_msg.shape)

    here = x * 2 + core

    def q_copy(step):
        peer = across(step)
        return remote(
            q_msg.at[pl.ds(peer // 2 * 2, 2)],
            q_land.at[here],
            (q_send, q_recv),
            number(step),
            to(tp_of((0, *step))),
        )

    pl.semaphore_wait(barrier, greetings)
    start(map(q_copy, X_CORE))
    loads[0].wait()
    loads[1].wait()
    each(0, SITE // 2, pack_and_send)
    each(SITE // 2, SITE, lambda i: pack_page(0, i))

    def near_copy(i):
        n = page_in_turn(i)
        return pltpu.make_async_copy(stage.at[SITE + n], near_hbm.at[n], near_sem.at[i])

    def pack_near(i):
        pack_page(1, i)
        near_copy(i).start()

    each(0, SITE, pack_near)
    for role in range(2):
        land[role * SITE + SITE - 1] = stage[role * SITE + SITE - 1]

    q_land[here] = q_msg[pl.ds(x * 2, 2)]
    arrive(map(q_copy, X_CORE))
    wide[: 2 * SITE * MSG] = q_land[...].reshape(2 * SITE * MSG, LANES).astype(F32)
    for i, c in itertools.product(range(2), range(BLOCKS)):
        halves = [wide[pl.ds(i * MSG + 2 * c + e, SITE, stride=2 * MSG), :] for e in range(2)]
        q_part[i, c] = jnp.concatenate(halves, axis=0).astype(BF16)

    def query_copy(role, dz):
        return remote(
            q_part.at[along(dz) // 2],
            q_all.at[role, z_hi],
            (all_send, all_recv),
            role * QUARTERS + dz,
            to(tp_of((dz, 0, 0)), z * n_y + (y + (1 - role) * sign * FAR + n_y) % n_y),
        )

    def part_copy(step):
        peer = tp_of(step)
        held = along(step[0]) * 8 + across(step[1:])
        return remote(
            part_msg.at[held], part_land.at[tp], (part_send, part_recv), number(step), to(peer)
        )

    def back_copy(rows=slice(None)):
        return remote(
            far_msg.at[rows], far_land.at[rows], (all_send, all_recv), 2 * QUARTERS, to(tp, place(z, y - sign * FAR))
        )

    start([query_copy(0, dz) for dz in Z_HI + [0]])
    start([query_copy(1, dz) for dz in Z_HI])
    q_all[1, z_hi] = q_part[z_hi // 2]
    each(SITE // 2, SITE, lambda i: send_page(0, i))

    def send_near(i):
        near_copy(i).wait()
        send_page(1, i)

    each(0, SITE, send_near)
    for load in loads[3:]:
        load.wait()

    lat = up_ref.shape[1]
    heads = 2 * n_tp
    transposed = (((1,), (1,)), ((), ()))

    def attend(role, first, count, last, before):
        group = z * n_y + (y - sign * (1 - role) * FAR + n_y) % n_y
        row = group * requests + request
        length = len_ref[row]

        lane = lax.broadcasted_iota(jnp.int32, (1, count * page_tokens), 1)
        dz, move = route(first + lane % (count * half) // half)
        source = (z + dz) % 2 * n_y + (y - sign * (1 - 2 * role) * move + n_y) % n_y
        limit = jnp.zeros_like(lane)
        for k in range(n_pool):
            holder = table_ref[k, row] >> 9
            limit = jnp.where(source == holder, length - (first_page + k) * page_tokens, limit)
        live = lane // (count * half) * half + lane % half < limit

        each(first, last, lambda n: page_copy(role, n).wait_recv())
        if before is None:
            arrive([query_copy(role, dz) for dz in Z_HI + [0] * (1 - role)])
        blocks = [
            jnp.concatenate([q_all[role, u, c] for u in range(QUARTERS)], axis=0)
            for c in range(BLOCKS)
        ]
        query = jnp.concatenate(blocks[:4], axis=1)
        rest = blocks[4][:, : LANES // 2]
        blank = jnp.zeros_like(rest)
        rest = jnp.concatenate(
            [jnp.concatenate([rest, blank], axis=1), jnp.concatenate([blank, rest], axis=1)], axis=0
        )
        block = land[pl.ds(role * SITE + first, count)]

        def rows(begin):
            return block[:, begin : begin + half].reshape(count * half, LANES)

        keys = jnp.concatenate(
            [
                jnp.concatenate([rows(c * page_tokens + h * half) for c in range(4)], axis=1)
                for h in range(2)
            ],
            axis=0,
        )
        scores = lax.dot_general(query, keys, transposed, preferred_element_type=F32)
        extra = lax.dot_general(rest, rows(4 * page_tokens), transposed, preferred_element_type=F32)
        scores += jnp.concatenate([extra[:heads], extra[heads:]], axis=1)
        scores = jnp.where(live, scores * score_scale, masked_score)
        top = jnp.broadcast_to(jnp.max(scores, axis=1, keepdims=True), (heads, LANES))
        if before is not None:
            top = jnp.maximum(top, before[0])
        weights = jnp.where(live, jnp.exp(scores - top[:, :1]), 0.0)
        total = jnp.broadcast_to(jnp.sum(weights, axis=1, keepdims=True), (heads, LANES))
        mixed = jnp.dot(weights.astype(BF16), keys, preferred_element_type=F32)
        if before is not None:
            scale = jnp.exp(before[0] - top)
            total += before[1] * scale
            mixed += before[2] * scale[:, :1]
        return top, total, mixed

    def normalised(top, total, mixed):
        some = total > 0.0
        safe = jnp.where(some, total, 1.0)
        inverse = 1.0 / safe
        return jnp.where(some, top + jnp.log(safe), masked_score), mixed * inverse[:, :1]

    first, second = core * CHUNK, (1 - core) * CHUNK
    state = attend(0, first, CHUNK, first + CHUNK - core, None)
    lse, even = normalised(*attend(0, second, CHUNK, second + CHUNK - (1 - core), state))
    for c in range(4):
        far_msg[c * heads : (c + 1) * heads] = even[:, c * LANES : (c + 1) * LANES].astype(BF16)
    lane = lax.broadcasted_iota(jnp.int32, (heads, LANES), 1)
    hi, mid, low = split3(lse)
    stat = jnp.where(lane == 0, hi, jnp.where(lane == 1, mid, jnp.where(lane == 2, low, 0.0)))
    far_msg[4 * heads :] = stat.astype(BF16)
    start([back_copy(pl.ds(c * heads, heads)) for c in range(BLOCKS)])

    state = attend(1, first, CHUNK, first + CHUNK - core, None)
    top, total, mixed = attend(1, second, CHUNK, second + CHUNK - (1 - core), state)
    back_copy().wait_recv()
    back = jnp.sum(far_land[4 * heads :].astype(F32), axis=1, keepdims=True)
    new_top = jnp.maximum(top, back)
    scale = jnp.exp(top - new_top)
    share = jnp.where(back > 0.5 * masked_score, jnp.exp(back - new_top), 0.0)
    mixed = jnp.concatenate(
        [
            mixed[:, c * LANES : (c + 1) * LANES] * scale
            + far_land[c * heads : (c + 1) * heads].astype(F32) * share
            for c in range(4)
        ],
        axis=1,
    )
    lse, even = normalised(new_top, total * scale + share, mixed)
    parts = split3(lse) + (jnp.zeros_like(lse),)
    for u, e in itertools.product(range(QUARTERS), range(2)):
        mine = slice(u * MSG + e * 8, u * MSG + e * 8 + 8)
        for c in range(4):
            row = u * 8 * MSG + 2 * c + e
            wide[pl.ds(row, 8, stride=MSG), :] = even[mine, c * LANES : (c + 1) * LANES]
            wide[pl.ds(row + 8, 8, stride=MSG), :] = parts[c][mine]
    part_msg[...] = wide[...].astype(BF16).reshape(part_msg.shape)
    part_copies = [part_copy(step) for step in TP]
    start(part_copies)
    part_land[tp] = part_msg[z_hi * 8 + here]
    arrive(part_copies)

    wide[...] = part_land[...].reshape(wide.shape).astype(F32)
    values = []
    for e in range(2):

        def rows(k, j):
            return wide[pl.ds(k * MSG + 2 * j + e, GROUPS, stride=QUARTERS * MSG), :]

        lses = [rows(k, 4) + rows(k, 5) + rows(k, 6) for k in range(QUARTERS)]
        best = functools.reduce(jnp.maximum, lses)
        share = [jnp.exp(one - best) for one in lses]
        norm = 1.0 / functools.reduce(jnp.add, share)
        attended = []
        for c in range(4):
            block = functools.reduce(jnp.add, [share[k] * rows(k, c) for k in range(QUARTERS)])
            attended.append((block * norm).astype(BF16))
        attended = jnp.concatenate(attended, axis=1)
        values.append(jnp.dot(attended, up_ref[e], preferred_element_type=F32))
    head_msg[...] = jnp.concatenate(values, axis=0).astype(BF16)

    def head_copy(step):
        return remote(
            head_msg, head_land.at[pool], (head_send, head_recv), number(step), to(tp, pool_of(step))
        )

    start(map(head_copy, POOL))
    head_land[pool] = head_msg[...]
    arrive(map(head_copy, POOL))

    landed = head_land[...].astype(F32)
    left = [landed[:, 8 * e : 8 * e + 8].reshape(4 * n_tp, LANES).astype(BF16) for e in range(2)]
    product = lax.dot_general(
        jnp.concatenate(left, axis=1), proj_ref[...], transposed, preferred_element_type=F32
    )
    columns = proj_ref.shape[0]
    blank = jnp.zeros((4 * n_tp, 4 * LANES - columns), F32)
    product = jnp.concatenate([product, blank], axis=1)
    for j in range(n_tp):
        last_msg[j] = product[4 * j : 4 * j + 4].astype(BF16)

    def last_copy(step):
        peer = tp_of(step)
        return remote(
            last_msg.at[peer], out_ref.at[tp], (last_send, last_recv), number(step), to(peer)
        )

    start(map(last_copy, TP))
    own = pltpu.make_async_copy(last_msg.at[tp], out_ref.at[tp], last_send.at[0])
    own.start()
    each(0, SITE - 1, lambda n: page_copy(0, n).wait_send())
    each(0, SITE - 1, lambda n: page_copy(1, n).wait_send())
    sent = [q_copy(step) for step in X_CORE]
    sent += [query_copy(0, dz) for dz in Z_HI + [0]] + [query_copy(1, dz) for dz in Z_HI]
    sent += [back_copy()] + part_copies
    sent += [head_copy(step) for step in POOL]
    sent += [last_copy(step) for step in TP]
    for copy in sent:
        copy.wait_send()
    own.wait()
    arrive(map(last_copy, TP))


def per_device(n_pool, n_tp, page_store, page_table, context_len, absorbed_query, value_up, out_proj):
    pages, tokens, key_width = page_store.shape
    requests = absorbed_query.shape[0]
    columns = out_proj.shape[1]
    hbm = pl.BlockSpec(memory_space=pltpu.HBM)
    message = lambda *lead: pltpu.VMEM((*lead, MSG, LANES), BF16)
    sems = lambda n: [pltpu.SemaphoreType.DMA((n,)), pltpu.SemaphoreType.DMA((n,))]
    packed_page = (tokens * key_width // LANES, LANES)
    summands, _ = pl.pallas_call(
        functools.partial(kernel, n_pool, n_tp),
        out_shape=[
            jax.ShapeDtypeStruct((n_tp, 4, 4 * LANES), BF16),
            jax.ShapeDtypeStruct((SITE, *packed_page), BF16),
        ],
        in_specs=[hbm] * 6,
        out_specs=[hbm, hbm],
        scratch_shapes=[
            pltpu.SMEM((n_pool, page_table.shape[0]), jnp.int32),
            pltpu.SMEM(context_len.shape, jnp.int32),
            pltpu.VMEM(page_store.shape, BF16),
            pltpu.VMEM(absorbed_query.shape, BF16),
            pltpu.VMEM(value_up.shape, BF16),
            pltpu.VMEM(out_proj.shape[::-1], BF16),
            pltpu.SemaphoreType.DMA((6,)),
            pltpu.SemaphoreType.DMA((SITE,)),
            pltpu.VMEM((n_pool, tokens * key_width // LANES, LANES), BF16),
            pltpu.VMEM((n_pool, tokens * key_width // LANES, LANES), BF16),
            message(GROUPS),
            message(SITE, 2),
            message(2, BLOCKS),
            message(2, QUARTERS, BLOCKS),
            pltpu.VMEM((BLOCKS * 2 * n_tp, LANES), BF16),
            pltpu.VMEM((BLOCKS * 2 * n_tp, LANES), BF16),
            message(n_tp),
            message(n_tp),
            message(),
            message(n_pool),
            pltpu.VMEM((n_tp, 4, 4 * LANES), BF16),
            pltpu.VMEM((n_tp * MSG, LANES), F32),
            *sems(2 * SITE),
            *sems(4 * SITE),
            *sems(2 * QUARTERS + 1),
            *sems(n_tp),
            *sems(2 * SITE),
            *sems(n_tp),
        ],
        compiler_params=pltpu.CompilerParams(
            collective_id=0, has_side_effects=True, vmem_limit_bytes=62 * 1024 * 1024
        ),
        name="mla_decode",
    )(page_table.T, context_len, page_store, absorbed_query, value_up, out_proj.T)
    return jnp.sum(summands.astype(F32), axis=0)[:, :columns].astype(BF16)


def solution(mesh):
    placed = (
        P(("pool", "tp"), None, None),
        P(),
        P(),
        P("pool", "tp", None),
        P("tp", None, None),
        P("tp", "pool"),
    )
    return jax.shard_map(
        functools.partial(per_device, mesh.shape["pool"], mesh.shape["tp"]),
        mesh=mesh,
        in_specs=placed,
        out_specs=P("tp", "pool"),
        check_vma=False,
    )
```

```python
import functools
import itertools

import jax
import jax.numpy as jnp
from jax import lax
from jax.experimental import pallas as pl
from jax.experimental.pallas import tpu as pltpu
from jax.sharding import PartitionSpec as P

MESH = pl.DeviceIdType.MESH
score_scale = 192.0 ** (-0.5)
masked_score = -1e30
F32 = jnp.float32
BF16 = jnp.bfloat16
LANES = 128
MSG = 16
CHUNK = 4
FAR = 3
SITE = 8
X_CORE = [(2, 1), (2, 0), (1, 1), (3, 1), (1, 0), (3, 0), (0, 1)]
Z_HI = [2, 1, 3]
TP = [(dz, dx, dc) for dz in (2, 1, 3, 0) for dx in (2, 1, 3, 0) for dc in (1, 0)][:-1]
POOL = [(dz, dy) for dy in (4, 3, 5, 2, 6, 1, 7) for dz in (1, 0)] + [(1, 0)]
SITES = [(dz, dy) for dz, dy in POOL if dy not in (3, 4, 5)]
QUARTERS = 4
GROUPS = 8
BLOCKS = 5


def split3(x):
    hi = x.astype(BF16).astype(F32)
    mid = (x - hi).astype(BF16).astype(F32)
    return hi, mid, x - hi - mid


def each(first, last, body):
    def step(i, carry):
        body(i)
        return carry

    lax.fori_loop(first, last, step, 0)


def kernel(
    n_pool,
    n_tp,
    table_hbm,
    len_hbm,
    store_hbm,
    query_hbm,
    up_hbm,
    proj_hbm,
    out_ref,
    table_ref,
    len_ref,
    store_ref,
    query_ref,
    up_ref,
    proj_ref,
    local_sem,
    stage,
    land,
    q_msg,
    q_land,
    q_part,
    q_all,
    far_msg,
    far_land,
    part_msg,
    part_land,
    head_msg,
    head_land,
    last_msg,
    wide,
    page_send,
    page_recv,
    q_send,
    q_recv,
    all_send,
    all_recv,
    part_send,
    part_recv,
    head_send,
    head_recv,
    last_send,
    last_recv,
):
    pool = lax.axis_index("pool")
    tp = lax.axis_index("tp")
    n_y = n_pool // 2
    z, y = pool // n_y, pool % n_y
    sign = 1 - 2 * z
    page_tokens = store_ref.shape[1]
    requests = query_hbm.shape[0]
    request, quarter = tp // QUARTERS, tp % QUARTERS
    x, z_hi, core = tp // 8, tp // 2 % 4, tp % 2
    first_page = quarter * n_pool

    def place(at_z, at_y):
        return at_z * n_y + (at_y + 2 * n_y) % n_y

    def across(step):
        dx, dc = step
        return (x + dx) % 4 * 2 + (core + dc) % 2

    def along(dz):
        return (z_hi + dz) % 4

    def tp_of(step):
        dz, dx, dc = step
        return (x + dx) % 4 * 8 + (z_hi + dz) % 4 * 2 + (core + dc) % 2

    def pool_of(step):
        dz, dy = step
        return (z + dz) % 2 * n_y + (y + dy) % n_y

    def number(step):
        return step[0] * 8 + (step[1] if len(step) == 2 else step[1] * 2 + step[2])

    def to(tp_index, pool_index=pool):
        return {"pool": pool_index, "tp": tp_index}

    barrier = pltpu.get_barrier_semaphore()
    loads = [
        pltpu.make_async_copy(source, target, local_sem.at[i])
        for i, (source, target) in enumerate(
            [
                (table_hbm.at[pl.ds(pl.multiple_of(first_page, 8), n_pool)], table_ref),
                (store_hbm, store_ref),
                (query_hbm, query_ref),
                (len_hbm, len_ref),
                (up_hbm, up_ref),
                (proj_hbm, proj_ref),
            ]
        )
    ]
    for load in (loads[2], loads[0], loads[1]):
        load.start()

    def greet(tp_index, pool_index=pool):
        device = to(tp_index, pool_index)
        pl.semaphore_signal(barrier, inc=1, device_id=device, device_id_type=MESH)

    for step in X_CORE:
        greet(tp_of((0, *step)))
    for step in SITES:
        greet(tp, pool_of(step))
    for ahead in (FAR, -FAR):
        for dz in Z_HI + [0]:
            greet(tp_of((dz, 0, 0)), place(z, y + ahead))
    for dz in Z_HI:
        greet(tp_of((dz, 0, 0)))
    greetings = len(X_CORE) + len(SITES) + 2 * QUARTERS + len(Z_HI)
    for load in loads[3:]:
        load.start()

    me = pool * n_tp + tp

    def slot_of(group):
        row = group * requests + request

        def look(k, found):
            entry = table_ref[k, row]
            return found + jnp.where(entry >> 4 == me, entry & 15, 0)

        return lax.fori_loop(0, n_pool, look, 0, unroll=True)

    half = page_tokens // 2

    def packed(target, slot):
        for c in range(4):
            target[c * page_tokens : (c + 1) * page_tokens] = store_ref[
                slot, :, c * LANES : (c + 1) * LANES
            ]
        rest = store_ref[slot, :, 4 * LANES :]
        target[4 * page_tokens :] = jnp.concatenate([rest[:half], rest[half:]], axis=1)

    def remote(source, target, sems, i, device):
        send, recv = sems
        return pltpu.make_async_remote_copy(
            src_ref=source,
            dst_ref=target,
            send_sem=send.at[i],
            recv_sem=recv.at[i],
            device_id=device,
            device_id_type=MESH,
        )

    def start(copies):
        for copy in copies:
            copy.start()

    def arrive(copies):
        for copy in copies:
            copy.wait_recv()

    def route(n):
        k = n % 4
        return 1 - n // 4, (6 + k + n // 4 * (k // 2) * (6 * k - 11)) % n_y

    def page_copy(role, n):
        dz, move = route(n)
        to_z = (z + dz) % 2
        direction = (1 - 2 * to_z) * (1 - 2 * role)
        return remote(
            stage.at[role * SITE + n],
            land.at[role * SITE + n],
            (page_send, page_recv),
            role * SITE + n,
            to(tp, to_z * n_y + (y + direction * move + n_y) % n_y),
        )

    def send_pages(role, first, last):
        def send(i):
            n = (i + core * (SITE // 2)) % SITE
            dz, move = route(n)
            to_z = (z + dz) % 2
            direction = 1 - 2 * to_z
            ahead = direction * (1 - 2 * role) * move - direction * (1 - role) * FAR
            packed(stage.at[role * SITE + n], slot_of(to_z * n_y + (y + ahead + 2 * n_y) % n_y))

            @pl.when(n < SITE - 1)
            def _():
                page_copy(role, n).start()

        each(first, last, send)
        if last == SITE:
            local = role * SITE + SITE - 1
            land[local] = stage[local]

    loads[2].wait()
    for i in range(requests):
        for c in range(BLOCKS):
            width = min(LANES, query_ref.shape[-1] - c * LANES)
            wide[i * MSG + 2 * c : i * MSG + 2 * c + 2, :width] = query_ref[
                i, :, c * LANES : c * LANES + width
            ].astype(F32)
        wide[i * MSG + 2 * BLOCKS - 2 : (i + 1) * MSG, LANES // 2 :] = jnp.zeros((8, LANES // 2), F32)
        wide[i * MSG + 2 * BLOCKS : (i + 1) * MSG, : LANES // 2] = jnp.zeros((6, LANES // 2), F32)
    q_msg[...] = wide[: requests * MSG].astype(BF16).reshape(q_msg.shape)

    here = x * 2 + core

    def q_copy(step):
        peer = across(step)
        return remote(
            q_msg.at[pl.ds(peer // 2 * 2, 2)],
            q_land.at[here],
            (q_send, q_recv),
            number(step),
            to(tp_of((0, *step))),
        )

    pl.semaphore_wait(barrier, greetings)
    start(map(q_copy, X_CORE))
    loads[0].wait()
    loads[1].wait()
    send_pages(0, 0, 5)

    q_land[here] = q_msg[pl.ds(x * 2, 2)]
    arrive(map(q_copy, X_CORE))
    wide[: 2 * SITE * MSG] = q_land[...].reshape(2 * SITE * MSG, LANES).astype(F32)
    for i, c in itertools.product(range(2), range(BLOCKS)):
        halves = [wide[pl.ds(i * MSG + 2 * c + e, SITE, stride=2 * MSG), :] for e in range(2)]
        q_part[i, c] = jnp.concatenate(halves, axis=0).astype(BF16)

    def query_copy(role, dz):
        return remote(
            q_part.at[along(dz) // 2],
            q_all.at[role, z_hi],
            (all_send, all_recv),
            role * QUARTERS + dz,
            to(tp_of((dz, 0, 0)), z * n_y + (y + (1 - role) * sign * FAR + n_y) % n_y),
        )

    def part_copy(step):
        peer = tp_of(step)
        held = along(step[0]) * 8 + across(step[1:])
        return remote(
            part_msg.at[held], part_land.at[tp], (part_send, part_recv), number(step), to(peer)
        )

    def back_copy(rows=slice(None)):
        return remote(
            far_msg.at[rows], far_land.at[rows], (all_send, all_recv), 2 * QUARTERS, to(tp, place(z, y - sign * FAR))
        )

    start([query_copy(0, dz) for dz in Z_HI + [0]])
    start([query_copy(1, dz) for dz in Z_HI])
    q_all[1, z_hi] = q_part[z_hi // 2]
    send_pages(0, 5, SITE)
    send_pages(1, 0, SITE)
    for load in loads[3:]:
        load.wait()

    lat = up_ref.shape[1]
    heads = 2 * n_tp
    transposed = (((1,), (1,)), ((), ()))

    def attend(role, first, count, last, before):
        group = z * n_y + (y - sign * (1 - role) * FAR + n_y) % n_y
        row = group * requests + request
        length = len_ref[row]

        lane = lax.broadcasted_iota(jnp.int32, (1, count * page_tokens), 1)
        dz, move = route(first + lane % (count * half) // half)
        source = (z + dz) % 2 * n_y + (y - sign * (1 - 2 * role) * move + n_y) % n_y
        limit = jnp.zeros_like(lane)
        for k in range(n_pool):
            holder = table_ref[k, row] >> 9
            limit = jnp.where(source == holder, length - (first_page + k) * page_tokens, limit)
        live = lane // (count * half) * half + lane % half < limit

        each(first, last, lambda n: page_copy(role, n).wait_recv())
        if before is None:
            arrive([query_copy(role, dz) for dz in Z_HI + [0] * (1 - role)])
        blocks = [
            jnp.concatenate([q_all[role, u, c] for u in range(QUARTERS)], axis=0)
            for c in range(BLOCKS)
        ]
        query = jnp.concatenate(blocks[:4], axis=1)
        rest = blocks[4][:, : LANES // 2]
        blank = jnp.zeros_like(rest)
        rest = jnp.concatenate(
            [jnp.concatenate([rest, blank], axis=1), jnp.concatenate([blank, rest], axis=1)], axis=0
        )
        block = land[pl.ds(role * SITE + first, count)]

        def rows(begin):
            return block[:, begin : begin + half].reshape(count * half, LANES)

        keys = jnp.concatenate(
            [
                jnp.concatenate([rows(c * page_tokens + h * half) for c in range(4)], axis=1)
                for h in range(2)
            ],
            axis=0,
        )
        scores = lax.dot_general(query, keys, transposed, preferred_element_type=F32)
        extra = lax.dot_general(rest, rows(4 * page_tokens), transposed, preferred_element_type=F32)
        scores += jnp.concatenate([extra[:heads], extra[heads:]], axis=1)
        scores = jnp.where(live, scores * score_scale, masked_score)
        top = jnp.broadcast_to(jnp.max(scores, axis=1, keepdims=True), (heads, LANES))
        if before is not None:
            top = jnp.maximum(top, before[0])
        weights = jnp.where(live, jnp.exp(scores - top[:, :1]), 0.0)
        total = jnp.broadcast_to(jnp.sum(weights, axis=1, keepdims=True), (heads, LANES))
        mixed = jnp.dot(weights.astype(BF16), keys, preferred_element_type=F32)
        if before is not None:
            scale = jnp.exp(before[0] - top)
            total += before[1] * scale
            mixed += before[2] * scale[:, :1]
        return top, total, mixed

    def normalised(top, total, mixed):
        some = total > 0.0
        safe = jnp.where(some, total, 1.0)
        inverse = 1.0 / safe
        return jnp.where(some, top + jnp.log(safe), masked_score), mixed * inverse[:, :1]

    first, second = core * CHUNK, (1 - core) * CHUNK
    state = attend(0, first, CHUNK, first + CHUNK - core, None)
    lse, even = normalised(*attend(0, second, CHUNK, second + CHUNK - (1 - core), state))
    for c in range(4):
        far_msg[c * heads : (c + 1) * heads] = even[:, c * LANES : (c + 1) * LANES].astype(BF16)
    lane = lax.broadcasted_iota(jnp.int32, (heads, LANES), 1)
    hi, mid, low = split3(lse)
    stat = jnp.where(lane == 0, hi, jnp.where(lane == 1, mid, jnp.where(lane == 2, low, 0.0)))
    far_msg[4 * heads :] = stat.astype(BF16)
    start([back_copy(pl.ds(c * heads, heads)) for c in range(BLOCKS)])

    state = attend(1, first, CHUNK, first + CHUNK - core, None)
    top, total, mixed = attend(1, second, CHUNK, second + CHUNK - (1 - core), state)
    back_copy().wait_recv()
    back = jnp.sum(far_land[4 * heads :].astype(F32), axis=1, keepdims=True)
    new_top = jnp.maximum(top, back)
    scale = jnp.exp(top - new_top)
    share = jnp.where(back > 0.5 * masked_score, jnp.exp(back - new_top), 0.0)
    mixed = jnp.concatenate(
        [
            mixed[:, c * LANES : (c + 1) * LANES] * scale
            + far_land[c * heads : (c + 1) * heads].astype(F32) * share
            for c in range(4)
        ],
        axis=1,
    )
    lse, even = normalised(new_top, total * scale + share, mixed)
    parts = split3(lse) + (jnp.zeros_like(lse),)
    for u, e in itertools.product(range(QUARTERS), range(2)):
        mine = slice(u * MSG + e * 8, u * MSG + e * 8 + 8)
        for c in range(4):
            row = u * 8 * MSG + 2 * c + e
            wide[pl.ds(row, 8, stride=MSG), :] = even[mine, c * LANES : (c + 1) * LANES]
            wide[pl.ds(row + 8, 8, stride=MSG), :] = parts[c][mine]
    part_msg[...] = wide[...].astype(BF16).reshape(part_msg.shape)
    part_copies = [part_copy(step) for step in TP]
    start(part_copies)
    part_land[tp] = part_msg[z_hi * 8 + here]
    arrive(part_copies)

    wide[...] = part_land[...].reshape(wide.shape).astype(F32)
    values = []
    for e in range(2):

        def rows(k, j):
            return wide[pl.ds(k * MSG + 2 * j + e, GROUPS, stride=QUARTERS * MSG), :]

        lses = [rows(k, 4) + rows(k, 5) + rows(k, 6) for k in range(QUARTERS)]
        best = functools.reduce(jnp.maximum, lses)
        share = [jnp.exp(one - best) for one in lses]
        norm = 1.0 / functools.reduce(jnp.add, share)
        attended = []
        for c in range(4):
            block = functools.reduce(jnp.add, [share[k] * rows(k, c) for k in range(QUARTERS)])
            attended.append((block * norm).astype(BF16))
        attended = jnp.concatenate(attended, axis=1)
        values.append(jnp.dot(attended, up_ref[e], preferred_element_type=F32))
    head_msg[...] = jnp.concatenate(values, axis=0).astype(BF16)

    def head_copy(step):
        return remote(
            head_msg, head_land.at[pool], (head_send, head_recv), number(step), to(tp, pool_of(step))
        )

    start(map(head_copy, POOL))
    head_land[pool] = head_msg[...]
    arrive(map(head_copy, POOL))

    landed = head_land[...].astype(F32)
    left = [landed[:, 8 * e : 8 * e + 8].reshape(4 * n_tp, LANES).astype(BF16) for e in range(2)]
    product = lax.dot_general(
        jnp.concatenate(left, axis=1), proj_ref[...], transposed, preferred_element_type=F32
    )
    columns = proj_ref.shape[0]
    blank = jnp.zeros((4 * n_tp, 4 * LANES - columns), F32)
    product = jnp.concatenate([product, blank], axis=1)
    for j in range(n_tp):
        last_msg[j] = product[4 * j : 4 * j + 4].astype(BF16)

    def last_copy(step):
        peer = tp_of(step)
        return remote(
            last_msg.at[peer], out_ref.at[tp], (last_send, last_recv), number(step), to(peer)
        )

    start(map(last_copy, TP))
    own = pltpu.make_async_copy(last_msg.at[tp], out_ref.at[tp], last_send.at[0])
    own.start()
    each(0, SITE - 1, lambda n: page_copy(0, n).wait_send())
    each(0, SITE - 1, lambda n: page_copy(1, n).wait_send())
    sent = [q_copy(step) for step in X_CORE]
    sent += [query_copy(0, dz) for dz in Z_HI + [0]] + [query_copy(1, dz) for dz in Z_HI]
    sent += [back_copy()] + part_copies
    sent += [head_copy(step) for step in POOL]
    sent += [last_copy(step) for step in TP]
    for copy in sent:
        copy.wait_send()
    own.wait()
    arrive(map(last_copy, TP))


def per_device(n_pool, n_tp, page_store, page_table, context_len, absorbed_query, value_up, out_proj):
    pages, tokens, key_width = page_store.shape
    requests = absorbed_query.shape[0]
    columns = out_proj.shape[1]
    hbm = pl.BlockSpec(memory_space=pltpu.HBM)
    message = lambda *lead: pltpu.VMEM((*lead, MSG, LANES), BF16)
    sems = lambda n: [pltpu.SemaphoreType.DMA((n,)), pltpu.SemaphoreType.DMA((n,))]
    summands = pl.pallas_call(
        functools.partial(kernel, n_pool, n_tp),
        out_shape=jax.ShapeDtypeStruct((n_tp, 4, 4 * LANES), BF16),
        in_specs=[hbm] * 6,
        out_specs=hbm,
        scratch_shapes=[
            pltpu.SMEM((n_pool, page_table.shape[0]), jnp.int32),
            pltpu.SMEM(context_len.shape, jnp.int32),
            pltpu.VMEM(page_store.shape, BF16),
            pltpu.VMEM(absorbed_query.shape, BF16),
            pltpu.VMEM(value_up.shape, BF16),
            pltpu.VMEM(out_proj.shape[::-1], BF16),
            pltpu.SemaphoreType.DMA((6,)),
            pltpu.VMEM((n_pool, tokens * key_width // LANES, LANES), BF16),
            pltpu.VMEM((n_pool, tokens * key_width // LANES, LANES), BF16),
            message(GROUPS),
            message(SITE, 2),
            message(2, BLOCKS),
            message(2, QUARTERS, BLOCKS),
            pltpu.VMEM((BLOCKS * 2 * n_tp, LANES), BF16),
            pltpu.VMEM((BLOCKS * 2 * n_tp, LANES), BF16),
            message(n_tp),
            message(n_tp),
            message(),
            message(n_pool),
            pltpu.VMEM((n_tp, 4, 4 * LANES), BF16),
            pltpu.VMEM((n_tp * MSG, LANES), F32),
            *sems(2 * SITE),
            *sems(4 * SITE),
            *sems(2 * QUARTERS + 1),
            *sems(n_tp),
            *sems(2 * SITE),
            *sems(n_tp),
        ],
        compiler_params=pltpu.CompilerParams(
            collective_id=0, has_side_effects=True, vmem_limit_bytes=62 * 1024 * 1024
        ),
        name="mla_decode",
    )(page_table.T, context_len, page_store, absorbed_query, value_up, out_proj.T)
    return jnp.sum(summands.astype(F32), axis=0)[:, :columns].astype(BF16)


def solution(mesh):
    placed = (
        P(("pool", "tp"), None, None),
        P(),
        P(),
        P("pool", "tp", None),
        P("tp", None, None),
        P("tp", "pool"),
    )
    return jax.shard_map(
        functools.partial(per_device, mesh.shape["pool"], mesh.shape["tp"]),
        mesh=mesh,
        in_specs=placed,
        out_specs=P("tp", "pool"),
        check_vma=False,
    )
```
